512 devices in a mesh: blk: 64 (over y_hi, z, core), head: 8 (over y_lo, x).
Axes of the slice: x: 4, y: 8 (y_hi: 4, y_lo: 2; y = y_hi * 2 + y_lo), z: 8, core: 2. Of those that a mesh axis runs over, the one named last changes fastest.
Arguments:
- queries: bfloat16 [8192, 4096], P(('blk', 'head')), may hold values from -8 to 8
- keys: bfloat16 [8192, 1024], P(('blk', 'head')), may hold values from -8 to 8
- values: bfloat16 [8192, 1024], P(('blk', 'head')), may hold values from -6 to 6
- outputs: bfloat16 [8192, 4096], P(('blk', 'head')), may hold values from -4 to 4
- grad_out: bfloat16 [8192, 4096], P(('blk', 'head')), may hold values from -6 to 6
- span_order: int32 [64], replicated, may hold values from 0 to 63, each once
Outputs:
- grad_queries: bfloat16 [8192, 4096], P(('blk', 'head'))
- grad_keys: bfloat16 [8192, 1024], P(('blk', 'head'))
- grad_values: bfloat16 [8192, 1024], P(('blk', 'head'))
The draws below stay inside these ranges and needn't reach their ends.
Inputs may be any that keep to these rules, and one draw needn't show every extreme that they name: Block k of 128 stored rows of every token array holds the sequence's span span_order[k]; each span once.
All inputs are finite; a program needn't handle non-finite values.
Results may differ from the reference program's by a relative error of at most 0.0051.
Values may be sent and summed in bfloat16 or wider, within the bound.
A program may use at most 64 MiB of HBM per device.

```python
import math
import jax
import jax.numpy as jnp
from jax import lax

QHEADS = 32
KVHEADS = 8
HEAD_DIM = 128
SPAN = 128
SEQ = 8192
N_BLK = 64


def draw_queries(key, part):
    key = jax.random.fold_in(key, 1)
    noise_key = jax.random.fold_in(key, 0)
    sample = jax.random.normal(noise_key, (SEQ, QHEADS, HEAD_DIM), jnp.float32)
    sample = jnp.clip(sample, -6.0, 6.0)
    return sample.reshape(SEQ, QHEADS * HEAD_DIM).astype(jnp.bfloat16)


def draw_keys(key, part):
    key = jax.random.fold_in(key, 2)
    noise_key = jax.random.fold_in(key, 0)
    sample = jax.random.normal(noise_key, (SEQ, KVHEADS, HEAD_DIM), jnp.float32)
    sample = jnp.clip(sample, -6.0, 6.0)
    return sample.reshape(SEQ, KVHEADS * HEAD_DIM).astype(jnp.bfloat16)


def block_levels(rng, shape, pieces, smallest, largest):
    def one(axis_at, shards_of):
        steps = jax.random.uniform(jax.random.fold_in(jax.random.fold_in(rng, 6), axis_at), (shards_of,), jnp.float32, smallest / len(pieces), largest / len(pieces))
        return jnp.repeat(jnp.exp(steps), shape[axis_at] // shards_of).reshape((-1,) + (1,) * (len(shape) - axis_at - 1))

    factor_of = one(*pieces[0])
    for cut in pieces[1:]:
        factor_of = factor_of * one(*cut)
    return factor_of


def noise(stream_key, dims, width, most, pieces=(), kind=jnp.bfloat16):
    loudness = block_levels(stream_key, dims, pieces, -0.22, 0.18) if pieces else 1.0
    array = jax.random.normal(stream_key, dims, jnp.float32) * width * loudness
    return jnp.minimum(jnp.maximum(array, -most), most).astype(kind)


def setup_inputs(seed: int = 0) -> dict:
    arg_keys = jax.random.split(jax.random.key(seed), 7)
    queries = draw_queries(jax.random.fold_in(arg_keys[6], 71), 0)
    keys = draw_keys(jax.random.fold_in(arg_keys[6], 71), 0)
    values = noise(arg_keys[2], (SEQ, KVHEADS * HEAD_DIM), 1.0, 6.0, ((0, 512),))
    outputs = noise(arg_keys[3], (SEQ, QHEADS * HEAD_DIM), 0.5, 4.0, ((0, 512),))
    grad_out = noise(arg_keys[4], (SEQ, QHEADS * HEAD_DIM), 1.0, 6.0, ((0, 512),))
    span_order = jax.random.permutation(arg_keys[5], N_BLK).astype(jnp.int32)
    return dict(queries=queries, keys=keys, values=values, outputs=outputs, grad_out=grad_out, span_order=span_order)


NEG = -1e+30

def reference(queries, keys, values, outputs, grad_out, span_order):
    group_size = QHEADS // KVHEADS
    inv_root = 1.0 / math.sqrt(HEAD_DIM)
    row_ids = jnp.arange(SEQ, dtype=jnp.int32)
    positions = (span_order[row_ids // SPAN] * SPAN + row_ids % SPAN).astype(jnp.int32)
    query_heads = jnp.moveaxis(queries.reshape(SEQ, KVHEADS, group_size, HEAD_DIM), 1, 0)
    output_heads = jnp.moveaxis(outputs.reshape(SEQ, KVHEADS, group_size, HEAD_DIM), 1, 0)
    grad_heads = jnp.moveaxis(grad_out.reshape(SEQ, KVHEADS, group_size, HEAD_DIM), 1, 0)
    key_heads = jnp.moveaxis(keys.reshape(SEQ, KVHEADS, HEAD_DIM), 1, 0)
    value_heads = jnp.moveaxis(values.reshape(SEQ, KVHEADS, HEAD_DIM), 1, 0)
    blocks = SEQ // SPAN

    def per_head(operands):
        query_h, output_h, grad_h, key_h, value_h = operands
        key_wide = key_h.astype(jnp.float32)
        value_wide = value_h.astype(jnp.float32)

        def per_block(running, block_ops):
            key_acc, value_acc = running
            query_b, output_b, grad_b, pos_b = block_ops
            query_wide = query_b.astype(jnp.float32)
            grad_wide = grad_b.astype(jnp.float32)
            output_wide = output_b.astype(jnp.float32)
            scores = jnp.einsum('tgd,ud->gtu', query_wide, key_wide) * inv_root
            visible = positions[None, :] <= pos_b[:, None]
            peak = lax.optimization_barrier(jnp.max(jnp.where(visible, scores, NEG), axis=-1))
            summed = lax.optimization_barrier(jnp.sum(jnp.where(visible, jnp.exp(scores - peak[..., None]), 0.0), axis=-1))
            log_total = peak + jnp.log(summed)
            probabilities = jnp.where(visible, jnp.exp(scores - log_total[..., None]), 0.0)
            rowdot = lax.optimization_barrier(jnp.sum(grad_wide * output_wide, axis=-1)).T
            dprobs = jnp.einsum('tgd,ud->gtu', grad_wide, value_wide)
            dscores = lax.optimization_barrier((probabilities * (dprobs - rowdot[..., None])).astype(jnp.bfloat16)).astype(jnp.float32)
            weights_low = lax.optimization_barrier(probabilities.astype(jnp.bfloat16)).astype(jnp.float32)
            grad_q = (jnp.einsum('gtu,ud->tgd', dscores, key_wide) * inv_root).astype(jnp.bfloat16)
            key_acc = key_acc + jnp.einsum('gtu,tgd->ud', dscores, query_wide)
            value_acc = value_acc + jnp.einsum('gtu,tgd->ud', weights_low, grad_wide)
            return ((key_acc, value_acc), grad_q)
        start_acc = (jnp.zeros((SEQ, HEAD_DIM), jnp.float32), jnp.zeros((SEQ, HEAD_DIM), jnp.float32))
        block_ops = (query_h.reshape(blocks, SPAN, group_size, HEAD_DIM), output_h.reshape(blocks, SPAN, group_size, HEAD_DIM), grad_h.reshape(blocks, SPAN, group_size, HEAD_DIM), positions.reshape(blocks, SPAN))
        (key_acc, value_acc), grad_q = lax.scan(per_block, start_acc, block_ops)
        grad_q = grad_q.reshape(SEQ, group_size, HEAD_DIM)
        return (grad_q, (key_acc * inv_root).astype(jnp.bfloat16), value_acc.astype(jnp.bfloat16))
    grad_q, grad_k, grad_v = lax.map(per_head, (query_heads, output_heads, grad_heads, key_heads, value_heads))
    grad_queries = jnp.moveaxis(grad_q, 0, 1).reshape(SEQ, QHEADS * HEAD_DIM)
    grad_keys = jnp.moveaxis(grad_k, 0, 1).reshape(SEQ, KVHEADS * HEAD_DIM)
    grad_values = jnp.moveaxis(grad_v, 0, 1).reshape(SEQ, KVHEADS * HEAD_DIM)
    return (grad_queries, grad_keys, grad_values)
```

```python
import math

import jax
import jax.numpy as jnp
from jax import lax
from jax.experimental import pallas as pl
from jax.experimental.pallas import tpu as pltpu
from jax.sharding import PartitionSpec as P

NX, NY, NZ, NC = 4, 8, 8, 2
ROWS = 16
HD = 128
GROUP = 4
W = GROUP * HD
NEG = -1e30
MESH = pl.DeviceIdType.MESH
F32 = jnp.float32
BF16 = jnp.bfloat16
INV_ROOT = 1.0 / math.sqrt(HD)
LOG2E = 1.4426950408889634


def near_first(n):
    order = [0]
    for step in range(1, n):
        if step not in order:
            order.append(step)
        if n - step not in order and n - step > 0:
            order.append(n - step)
    return order


def dot_nt(a, b):
    return lax.dot_general(a, b, (((1,), (1,)), ((), ())), preferred_element_type=F32)


def dot_nn(a, b):
    return lax.dot_general(a, b, (((1,), (0,)), ((), ())), preferred_element_type=F32)


def dot_tn(a, b):
    return lax.dot_general(a, b, (((0,), (0,)), ((), ())), preferred_element_type=F32)


def kernel(
    q_in, k_in, v_in, o_in, g_in, order,
    q_out, k_out, v_out,
    o_buf, g_buf, r_buf, qd, kv, pos_u, pos_t, e_buf, dp_buf, m_buf, st, lse,
    dq_acc, dq_send, dq_recv, sib_send, sib_recv, y_send, y_recv, own_dkv, dq_fin, dkv_fin,
    loc_sem, a_send, a_recv, x_send, x_recv, f_send, f_recv, kvr_send, kvr_recv, kvl_send, kvl_recv,
    ks_send, ks_recv, st_send, st_recv, sb_send, sb_recv, yd_send, yd_recv, xd_send, xd_recv, zo_send, zo_recv,
):
    T = NZ * ROWS
    NJ = NC * NY // 2
    NP = NY // 2
    blk = lax.axis_index("blk")
    sub = lax.axis_index("head")
    core = blk % NC
    z = (blk // NC) % NZ
    yh = blk // (NC * NZ)
    x = sub % NX
    yl = sub // NX
    y = yh * 2 + yl
    slot = core * NY + y

    def dev(xx, yy, zz, cc):
        return ((yy // 2) * (NZ * NC) + zz * NC + cc, (yy % 2) * NX + xx)

    def at_x(d):
        return dev((x + d) % NX, y, z, core)

    def at_y(d):
        return dev(x, (y + d) % NY, z, core)

    def at_z(d):
        return dev(x, y, (z + d) % NZ, core)

    sibling = dev(x, y, z, (core + 1) % NC)

    def remote(src, dst, send_sem, recv_sem, who):
        return pltpu.make_async_remote_copy(
            src_ref=src, dst_ref=dst, send_sem=send_sem, recv_sem=recv_sem, device_id=who, device_id_type=MESH
        )

    def zrow(index):
        return pl.ds(pl.multiple_of(index * ROWS, ROWS), ROWS)

    def zcol(index, width):
        return pl.ds(pl.multiple_of(index * width, width), width)

    local = [
        pltpu.make_async_copy(o_in, o_buf, loc_sem.at[0]),
        pltpu.make_async_copy(g_in, g_buf, loc_sem.at[1]),
        pltpu.make_async_copy(k_in.at[:, zcol(z, HD)], kv.at[0, slot, zrow(z), :], loc_sem.at[2]),
        pltpu.make_async_copy(v_in.at[:, zcol(z, HD)], kv.at[1, slot, zrow(z), :], loc_sem.at[3]),
        pltpu.make_async_copy(q_in.at[:, zcol(z, W)], qd.at[x, zrow(z), pl.ds(0, W)], loc_sem.at[4]),
        pltpu.make_async_copy(g_in.at[:, zcol(z, W)], qd.at[x, zrow(z), pl.ds(W, W)], loc_sem.at[5]),
    ]
    for copy in local:
        copy.start()

    barrier = pltpu.get_barrier_semaphore()
    peers = [at_z(d) for d in range(1, NZ)] + [at_x(d) for d in range(1, NX)] + [at_y(d) for d in range(1, NY)]
    if NC == 2:
        peers.append(sibling)
    for who in peers:
        pl.semaphore_signal(barrier, inc=1, device_id=who, device_id_type=MESH)
    pl.semaphore_wait(barrier, len(peers))

    z_order = near_first(NZ)

    def a_copy(kind, d):
        to = (z + d) % NZ
        src, dst = {
            0: (k_in.at[:, zcol(to, HD)], kv.at[0, slot, zrow(z), :]),
            1: (v_in.at[:, zcol(to, HD)], kv.at[1, slot, zrow(z), :]),
            2: (q_in.at[:, zcol(to, W)], qd.at[x, zrow(z), pl.ds(0, W)]),
            3: (g_in.at[:, zcol(to, W)], qd.at[x, zrow(z), pl.ds(W, W)]),
            4: (r_buf.at[to], qd.at[x, zrow(z), pl.ds(2 * W, HD)]),
        }[kind]
        return remote(src, dst, a_send.at[kind, d], a_recv.at[kind, d], at_z(d))

    def a_arrived(kind, d):
        row = zrow((z + NZ - d) % NZ)
        ref = {
            0: kv.at[0, slot, row, :],
            1: kv.at[1, slot, row, :],
            2: qd.at[x, row, pl.ds(0, W)],
            3: qd.at[x, row, pl.ds(W, W)],
            4: qd.at[x, row, pl.ds(2 * W, HD)],
        }[kind]
        remote(ref, ref, a_send.at[kind, d], a_recv.at[kind, d], at_z(d)).wait_recv()

    for d in z_order[1:]:
        a_copy(0, d).start()
        a_copy(1, d).start()
    for d in z_order[1:]:
        a_copy(2, d).start()
        a_copy(3, d).start()

    local[0].wait()
    local[1].wait()
    lane = lax.broadcasted_iota(jnp.int32, (ROWS, HD), 1)

    def rowdots(zz, carry):
        spread = jnp.zeros((ROWS, HD), F32)
        for h in range(GROUP):
            cols = pl.ds(pl.multiple_of(zz * W + h * HD, HD), HD)
            dots = jnp.sum(g_buf[:, cols].astype(F32) * o_buf[:, cols].astype(F32), axis=1, keepdims=True)
            spread = jnp.where(lane // 32 == h, dots, spread)
        high = spread.astype(BF16).astype(F32)
        rest = spread - high
        middle = rest.astype(BF16).astype(F32)
        low = rest - middle
        piece = lane % 32
        pieces = jnp.where(piece == 0, high, jnp.where(piece == 1, middle, jnp.where(piece == 2, low, 0.0)))
        r_buf[zz] = pieces.astype(BF16)
        return carry

    lax.fori_loop(0, NZ, rowdots, 0)
    for d in z_order[1:]:
        a_copy(4, d).start()
    qd[x, zrow(z), pl.ds(2 * W, HD)] = r_buf[z]

    row_in = lax.broadcasted_iota(jnp.int32, (ROWS, HD), 0)
    for cc in range(NC):
        for yy in range(NY):
            for zz in range(NZ):
                base = order[(yy // 2) * (NZ * NC) + zz * NC + cc] * 128 + ((yy % 2) * NX + x) * ROWS
                pos_u[cc * NY + yy, pl.ds(zz * ROWS, ROWS), :] = row_in + base
    t_lane = lax.broadcasted_iota(jnp.int32, (8, T), 1)
    row_pos = jnp.zeros((8, T), jnp.int32)
    for zz in range(NZ):
        base = order[yh * (NZ * NC) + zz * NC + core] * 128 + yl * NX * ROWS
        row_pos = jnp.where(t_lane // ROWS == zz, base + t_lane % ROWS, row_pos)
    pos_t[...] = row_pos

    n_right, n_left = NY // 2, NY - 1 - NY // 2

    def kv_block(d):
        ref = kv.at[:, core * NY + (y + d + NY) % NY]
        return ref

    def right_copy(s):
        ref = kv_block(-s)
        return remote(ref, ref, kvr_send.at[s], kvr_recv.at[s], at_y(1))

    def left_copy(s):
        ref = kv_block(s)
        return remote(ref, ref, kvl_send.at[s], kvl_recv.at[s], at_y(NY - 1))

    def core_copy(d):
        ref = kv_block(d)
        return remote(ref, ref, ks_send.at[d % NY], ks_recv.at[d % NY], sibling)

    def kv_step(s):
        if s > 0:
            if s <= n_right:
                ref = kv_block(-s)
                remote(ref, ref, kvr_send.at[s - 1], kvr_recv.at[s - 1], at_y(1)).wait_recv()
            if s <= n_left:
                ref = kv_block(s)
                remote(ref, ref, kvl_send.at[s - 1], kvl_recv.at[s - 1], at_y(NY - 1)).wait_recv()
        if s < n_right:
            right_copy(s).start()
        if s < n_left:
            left_copy(s).start()
        if NC == 2:
            if s <= n_right:
                core_copy(-s).start()
            if 0 < s <= n_left:
                core_copy(s).start()

    local[2].wait()
    local[3].wait()
    for d in z_order[1:]:
        a_arrived(0, d)
        a_arrived(1, d)
    kv_step(0)

    half = (NZ + 1) // 2

    def x_piece(dx, d):
        return qd.at[(x + dx + NX) % NX, zrow((z + NZ - d) % NZ), :]

    def x_copy(way, d):
        ref = x_piece(0, d)
        return remote(ref, ref, x_send.at[way, d], x_recv.at[way, d], at_x(1 if way == 0 else NX - 1))

    def x_arrived(way, d):
        ref = x_piece(-1 if way == 0 else 1, d)
        remote(ref, ref, x_send.at[way, d], x_recv.at[way, d], at_x(1)).wait_recv()

    def far_copy(d):
        way = 0 if d < half else 1
        ref = x_piece(-1 if way == 0 else 1, d)
        return remote(ref, ref, f_send.at[d], f_recv.at[d], at_x(1 if way == 0 else NX - 1))

    def far_arrived(d):
        ref = x_piece(2, d)
        remote(ref, ref, f_send.at[d], f_recv.at[d], at_x(1)).wait_recv()

    def forward(d):
        x_arrived(0, d)
        x_arrived(1, d)
        far_copy(d).start()

    local[4].wait()
    local[5].wait()
    kv_steps = list(range(1, max(n_right, n_left) + 1))
    for i, d in enumerate(z_order):
        if d > 0:
            for kind in (2, 3, 4):
                a_arrived(kind, d)
        x_copy(0, d).start()
        x_copy(1, d).start()
        if i >= 2:
            forward(z_order[i - 2])
        if i % 2 == 1 and kv_steps:
            kv_step(kv_steps.pop(0))
    for s in kv_steps:
        kv_step(s)
    for d in z_order[max(0, NZ - 2):]:
        forward(d)
    if NC == 2:
        for d in range(NY):
            ref = kv.at[:, ((core + 1) % NC) * NY + (y + d) % NY]
            remote(ref, ref, ks_send.at[d], ks_recv.at[d], sibling).wait_recv()

    scale = INV_ROOT * LOG2E

    def stack_heads(ref, xs, first):
        return jnp.concatenate([ref[xs, :, first + h * HD:first + (h + 1) * HD] for h in range(GROUP)], axis=0)

    def key_rows(which, j):
        return kv[which, pl.ds(2 * j, 2)].reshape(2 * T, HD)

    def score_part(xs):
        queries = stack_heads(qd, xs, 0)
        t_pos = pos_t[0:1, :] + xs * ROWS

        def body(j, running):
            run_max, run_sum = running
            s = dot_nt(key_rows(0, j), queries)
            seen = pos_u[pl.ds(2 * j, 2)].reshape(2 * T, HD)[:, :T] <= t_pos
            tops, sums = [], []
            for h in range(GROUP):
                part = jnp.where(seen, s[:, h * T:(h + 1) * T] * scale, NEG)
                top = jnp.max(part, axis=0, keepdims=True)
                e = jnp.exp2(part - top)
                e_buf[j, xs, :, h * T:(h + 1) * T] = e
                tops.append(top)
                sums.append(jnp.sum(e, axis=0, keepdims=True))
            top = jnp.concatenate(tops, axis=1)
            total = jnp.concatenate(sums, axis=1)
            m_buf[j, xs] = top
            new_max = jnp.maximum(run_max, top)
            new_sum = run_sum * jnp.exp2(run_max - new_max) + total * jnp.exp2(top - new_max)
            return new_max, new_sum

        start = (jnp.full((1, GROUP * T), NEG, F32), jnp.zeros((1, GROUP * T), F32))
        run_max, run_sum = lax.fori_loop(0, NJ, body, start)
        st[x, xs, 0:1, :] = run_max
        st[x, xs, 1:2, :] = run_sum

    pick_row = lax.broadcasted_iota(jnp.int32, (8, HD), 0)
    pick_lane = lax.broadcasted_iota(jnp.int32, (8, HD), 1)
    pick = jnp.where((pick_lane // 32 == pick_row) & (pick_lane % 32 < 3), 1.0, 0.0).astype(BF16)

    def dprobs_part(xs):
        cotangents = stack_heads(qd, xs, W)
        rowdot = dot_nt(pick, qd[xs, :, 2 * W:])
        rowdot = jnp.concatenate([rowdot[h:h + 1, :] for h in range(GROUP)], axis=1)

        def body(j, carry):
            dp_buf[j, xs] = dot_nt(key_rows(1, j), cotangents) - rowdot
            return carry

        lax.fori_loop(0, NJ, body, 0)

    for dx in (0, NX - 1, 1):
        score_part((x + dx) % NX)
        dprobs_part((x + dx) % NX)
    for d in z_order:
        far_arrived(d)
    score_part((x + 2) % NX)

    def st_copy(d):
        return remote(st.at[x], st.at[x], st_send.at[d], st_recv.at[d], at_x(d))

    for d in range(1, NX):
        st_copy(d).start()
    dprobs_part((x + 2) % NX)
    for d in range(1, NX):
        ref = st.at[(x + NX - d) % NX]
        remote(ref, ref, st_send.at[d], st_recv.at[d], at_x(d)).wait_recv()
    for xs in range(NX):
        top = st[0, xs, 0:1, :]
        for other in range(1, NX):
            top = jnp.maximum(top, st[other, xs, 0:1, :])
        total = jnp.zeros((1, GROUP * T), F32)
        for other in range(NX):
            total = total + st[other, xs, 1:2, :] * jnp.exp2(st[other, xs, 0:1, :] - top)
        lse[xs] = top + jnp.log2(total)
    dq_acc[...] = jnp.zeros_like(dq_acc)

    def grad_chunk(j):
        keys = key_rows(0, j)
        dk = jnp.zeros((2 * T, HD), F32)
        dv = jnp.zeros((2 * T, HD), F32)
        for xs in range(NX):
            p = e_buf[j, xs] * jnp.exp2(m_buf[j, xs] - lse[xs])
            ds = (p * dp_buf[j, xs]).astype(BF16)
            dk = dk + dot_nn(ds, stack_heads(qd, xs, 0))
            dv = dv + dot_nn(p.astype(BF16), stack_heads(qd, xs, W))
            dq_acc[xs] += dot_tn(keys, ds)
        return dk, dv

    def sib_copy(p):
        return remote(sib_send.at[p], sib_recv.at[p], sb_send.at[p], sb_recv.at[p], sibling)

    if NC == 2:

        def other_core(p, carry):
            dk, dv = grad_chunk(((core + 1) % NC) * NP + p)
            sib_send[p, 0] = dk.astype(BF16)
            sib_send[p, 1] = dv.astype(BF16)
            sib_copy(p).start()
            return carry

        lax.fori_loop(0, NP, other_core, 0)

    def y_copy(p, half_of):
        d = (2 * p + half_of - y + 2 * NY) % NY
        src = y_send.at[p, :, pl.ds(pl.multiple_of(half_of * T, T), T), :]
        return remote(src, y_recv.at[d], yd_send.at[d], yd_recv.at[d], at_y(d))

    def own_core(p):
        dk, dv = grad_chunk(core * NP + p)
        if NC == 2:
            sib_copy(p).wait_recv()
            dk = dk + sib_recv[p, 0].astype(F32)
            dv = dv + sib_recv[p, 1].astype(F32)
        y_send[p, 0] = dk.astype(BF16)
        y_send[p, 1] = dv.astype(BF16)
        return dk, dv

    far_pairs = [NP // 2] + [d for d in range(1, NP) if d != NP // 2] if NP > 1 else []

    def far_pair(i, carry):
        p = (yh + (NP // 2 + i) % (NP - 1) + 1) % NP if NP > 2 else (yh + 1) % NP
        own_core(p)
        y_copy(p, 0).start()
        y_copy(p, 1).start()
        return carry

    if far_pairs:
        lax.fori_loop(0, NP - 1, far_pair, 0)
    dk, dv = own_core(yh)
    own_dkv[0] = dk
    own_dkv[1] = dv
    y_copy(yh, 1 - yl).start()

    def dq_copy(d):
        to = (x + d) % NX
        return remote(dq_send.at[to], dq_recv.at[d], xd_send.at[d], xd_recv.at[d], at_x(d))

    dq_send[...] = dq_acc[...].astype(BF16)
    for d in (2, 1, 3):
        dq_copy(d).start()

    def out_copy(kind, d):
        to = (z + d) % NZ
        src, dst = {
            0: (dq_fin.at[zrow(to), :], q_out.at[:, zcol(z, W)]),
            1: (dkv_fin.at[0, zrow(to), :], k_out.at[:, zcol(z, HD)]),
            2: (dkv_fin.at[1, zrow(to), :], v_out.at[:, zcol(z, HD)]),
        }[kind]
        if d == 0:
            return pltpu.make_async_copy(src, dst, zo_send.at[kind, 0])
        return remote(src, dst, zo_send.at[kind, d], zo_recv.at[kind, d], at_z(d))

    own_rows = pl.ds(pl.multiple_of(yl * T, T), T)
    sums = [own_dkv[0, own_rows, :], own_dkv[1, own_rows, :]]
    for d in range(1, NY):
        ref = y_recv.at[d]
        remote(ref, ref, yd_send.at[d], yd_recv.at[d], at_y(d)).wait_recv()
        sums = [sums[i] + y_recv[d, i].astype(F32) for i in range(2)]
    dkv_fin[0] = (sums[0] * INV_ROOT).astype(BF16)
    dkv_fin[1] = sums[1].astype(BF16)
    for d in z_order:
        out_copy(1, d).start()
        out_copy(2, d).start()

    dq = dq_acc[x]
    for d in range(1, NX):
        ref = dq_recv.at[d]
        remote(ref, ref, xd_send.at[d], xd_recv.at[d], at_x(d)).wait_recv()
        dq = dq + dq_recv[d].astype(F32)
    dq = dq * INV_ROOT
    for h in range(GROUP):
        dq_fin[:, h * HD:(h + 1) * HD] = dq[:, h * T:(h + 1) * T].T.astype(BF16)
    for d in z_order:
        out_copy(0, d).start()

    for kind in range(3):
        out_copy(kind, 0).wait()
    for d in z_order[1:]:
        src = (z + NZ - d) % NZ
        for kind, ref in (
            (0, q_out.at[:, zcol(src, W)]),
            (1, k_out.at[:, zcol(src, HD)]),
            (2, v_out.at[:, zcol(src, HD)]),
        ):
            remote(ref, ref, zo_send.at[kind, d], zo_recv.at[kind, d], at_z(d)).wait_recv()
    for d in z_order[1:]:
        for kind in range(5):
            a_copy(kind, d).wait_send()
        for kind in range(3):
            out_copy(kind, d).wait_send()
    for d in range(NZ):
        x_copy(0, d).wait_send()
        x_copy(1, d).wait_send()
        far_copy(d).wait_send()
    for s in range(n_right):
        right_copy(s).wait_send()
    for s in range(n_left):
        left_copy(s).wait_send()
    if NC == 2:
        for d in range(NY):
            core_copy(d).wait_send()
        for p in range(NP):
            sib_copy(p).wait_send()
    for d in range(1, NX):
        st_copy(d).wait_send()
        dq_copy(d).wait_send()
    for d in range(1, NY):
        ref = y_recv.at[d]
        remote(ref, ref, yd_send.at[d], yd_recv.at[d], at_y(d)).wait_send()


def on_device(queries, keys, values, outputs, grad_out, span_order):
    T = NZ * ROWS
    NJ = NC * NY // 2
    NP = NY // 2
    QW = 2 * W + HD
    vmem = pltpu.VMEM
    dma = pltpu.SemaphoreType.DMA
    width = W * NZ
    kv_width = HD * NZ
    scratch = [
        vmem((ROWS, width), BF16),
        vmem((ROWS, width), BF16),
        vmem((NZ, ROWS, HD), BF16),
        vmem((NX, T, QW), BF16),
        vmem((2, NC * NY, T, HD), BF16),
        vmem((NC * NY, T, HD), jnp.int32),
        vmem((8, T), jnp.int32),
        vmem((NJ, NX, 2 * T, GROUP * T), F32),
        vmem((NJ, NX, 2 * T, GROUP * T), F32),
        vmem((NJ, NX, 1, GROUP * T), F32),
        vmem((NX, NX, 2, GROUP * T), F32),
        vmem((NX, 1, GROUP * T), F32),
        vmem((NX, HD, GROUP * T), F32),
        vmem((NX, HD, GROUP * T), BF16),
        vmem((NX, HD, GROUP * T), BF16),
        vmem((NP, 2, 2 * T, HD), BF16),
        vmem((NP, 2, 2 * T, HD), BF16),
        vmem((NP, 2, 2 * T, HD), BF16),
        vmem((NY, 2, T, HD), BF16),
        vmem((2, 2 * T, HD), F32),
        vmem((T, W), BF16),
        vmem((2, T, HD), BF16),
        dma((6,)),
        dma((5, NZ)), dma((5, NZ)),
        dma((2, NZ)), dma((2, NZ)),
        dma((NZ,)), dma((NZ,)),
        dma((NY,)), dma((NY,)),
        dma((NY,)), dma((NY,)),
        dma((NY,)), dma((NY,)),
        dma((NX,)), dma((NX,)),
        dma((NP,)), dma((NP,)),
        dma((NY,)), dma((NY,)),
        dma((NX,)), dma((NX,)),
        dma((3, NZ)), dma((3, NZ)),
    ]
    anywhere = pl.BlockSpec(memory_space=pl.ANY)
    return pl.pallas_call(
        kernel,
        out_shape=(
            jax.ShapeDtypeStruct((ROWS, width), BF16),
            jax.ShapeDtypeStruct((ROWS, kv_width), BF16),
            jax.ShapeDtypeStruct((ROWS, kv_width), BF16),
        ),
        in_specs=[anywhere] * 5 + [pl.BlockSpec(memory_space=pltpu.SMEM)],
        out_specs=(anywhere, anywhere, anywhere),
        scratch_shapes=scratch,
        compiler_params=pltpu.CompilerParams(
            collective_id=0, has_side_effects=True, vmem_limit_bytes=60 * 1024 * 1024
        ),
    )(queries, keys, values, outputs, grad_out, span_order)


def solution(mesh):
    rows = P(("blk", "head"), None)
    return jax.shard_map(
        on_device,
        mesh=mesh,
        in_specs=(rows, rows, rows, rows, rows, P()),
        out_specs=(rows, rows, rows),
        check_vma=False,
    )
```

```python
import math

import jax
import jax.numpy as jnp
from jax import lax
from jax.experimental import pallas as pl
from jax.experimental.pallas import tpu as pltpu
from jax.sharding import PartitionSpec as P

NX, NY, NZ, NC = 4, 8, 8, 2
ROWS = 16
HD = 128
GROUP = 4
W = GROUP * HD
NEG = -1e30
MESH = pl.DeviceIdType.MESH
F32 = jnp.float32
BF16 = jnp.bfloat16
INV_ROOT = 1.0 / math.sqrt(HD)
LOG2E = 1.4426950408889634


def near_first(n):
    order = [0]
    for step in range(1, n):
        if step not in order:
            order.append(step)
        if n - step not in order and n - step > 0:
            order.append(n - step)
    return order


def dot_nt(a, b):
    return lax.dot_general(a, b, (((1,), (1,)), ((), ())), preferred_element_type=F32)


def dot_nn(a, b):
    return lax.dot_general(a, b, (((1,), (0,)), ((), ())), preferred_element_type=F32)


def dot_tn(a, b):
    return lax.dot_general(a, b, (((0,), (0,)), ((), ())), preferred_element_type=F32)


def kernel(
    q_in, k_in, v_in, o_in, g_in, order,
    q_out, k_out, v_out,
    o_buf, g_buf, r_buf, r_own, rd_buf, qg, kv, pos_u, pos_t, qt_buf, gt_buf, kt_buf, e_buf, dp_buf, ds_buf, m_buf, l_buf, st, lse,
    dq_own, dq_send, dq_recv, sib_send, sib_recv, y_send, y_recv, own_dkv, dq_fin, dkv_fin,
    loc_sem, a_send, a_recv, x_send, x_recv, rd_send, rd_recv, kv_send, kv_recv,
    ks_send, ks_recv, st_send, st_recv, sb_send, sb_recv, yd_send, yd_recv, xd_send, xd_recv, zo_send, zo_recv,
):
    T = NZ * ROWS
    NJ = NC * NY // 2
    NP = NY // 2
    blk = lax.axis_index("blk")
    sub = lax.axis_index("head")
    core = blk % NC
    z = (blk // NC) % NZ
    yh = blk // (NC * NZ)
    x = sub % NX
    yl = sub // NX
    y = yh * 2 + yl
    slot = core * NY + y

    def dev(xx, yy, zz, cc):
        return ((yy // 2) * (NZ * NC) + zz * NC + cc, (yy % 2) * NX + xx)

    def at_x(d):
        return dev((x + d) % NX, y, z, core)

    def at_y(d):
        return dev(x, (y + d) % NY, z, core)

    def at_z(d):
        return dev(x, y, (z + d) % NZ, core)

    sibling = dev(x, y, z, (core + 1) % NC)

    def remote(src, dst, send_sem, recv_sem, who):
        return pltpu.make_async_remote_copy(
            src_ref=src, dst_ref=dst, send_sem=send_sem, recv_sem=recv_sem, device_id=who, device_id_type=MESH
        )

    def zrow(index):
        return pl.ds(pl.multiple_of(index * ROWS, ROWS), ROWS)

    def zcol(index, width):
        return pl.ds(pl.multiple_of(index * width, width), width)

    barrier = pltpu.get_barrier_semaphore()
    peers = [at_z(d) for d in near_first(NZ)[:0:-1]] + [at_y(d) for d in near_first(NY)[:0:-1]]
    peers += [at_x(d) for d in range(1, NX)]
    if NC == 2:
        peers.append(sibling)
    for who in peers:
        pl.semaphore_signal(barrier, inc=1, device_id=who, device_id_type=MESH)

    local = [
        pltpu.make_async_copy(o_in, o_buf, loc_sem.at[0]),
        pltpu.make_async_copy(g_in, g_buf, loc_sem.at[1]),
        pltpu.make_async_copy(q_in.at[:, zcol(z, W)], qg.at[0, x, zrow(z), :], loc_sem.at[2]),
        pltpu.make_async_copy(g_in.at[:, zcol(z, W)], qg.at[1, x, zrow(z), :], loc_sem.at[3]),
        pltpu.make_async_copy(k_in.at[:, zcol(z, HD)], kv.at[0, slot, zrow(z), :], loc_sem.at[4]),
        pltpu.make_async_copy(v_in.at[:, zcol(z, HD)], kv.at[1, slot, zrow(z), :], loc_sem.at[5]),
    ]
    for copy in local:
        copy.start()

    pl.semaphore_wait(barrier, len(peers))

    z_order = near_first(NZ)
    y_order = near_first(NY)

    def a_copy(kind, d):
        to = (z + d) % NZ
        src, dst = {
            0: (k_in.at[:, zcol(to, HD)], kv.at[0, slot, zrow(z), :]),
            1: (v_in.at[:, zcol(to, HD)], kv.at[1, slot, zrow(z), :]),
            2: (q_in.at[:, zcol(to, W)], qg.at[0, x, zrow(z), :]),
            3: (g_in.at[:, zcol(to, W)], qg.at[1, x, zrow(z), :]),
            4: (r_buf.at[to], r_own.at[zrow(z), :]),
        }[kind]
        return remote(src, dst, a_send.at[kind, d], a_recv.at[kind, d], at_z(d))

    def a_arrived(kind, d):
        row = zrow((z + NZ - d) % NZ)
        ref = {
            0: kv.at[0, slot, row, :],
            1: kv.at[1, slot, row, :],
            2: qg.at[0, x, row, :],
            3: qg.at[1, x, row, :],
            4: r_own.at[row, :],
        }[kind]
        remote(ref, ref, a_send.at[kind, d], a_recv.at[kind, d], at_z(d)).wait_recv()

    def x_copy(kind, dx, d):
        ref = qg.at[kind, x, zrow((z + NZ - d) % NZ), :]
        return remote(ref, ref, x_send.at[kind, dx, d], x_recv.at[kind, dx, d], at_x(dx))

    def x_arrived(kind, dx, d):
        ref = qg.at[kind, (x + NX - dx) % NX, zrow((z + NZ - d) % NZ), :]
        remote(ref, ref, x_send.at[kind, dx, d], x_recv.at[kind, dx, d], at_x(dx)).wait_recv()

    def x_piece(kind, d):
        if d > 0:
            a_arrived(2 + kind, d)
        for dx in (2, 1, 3):
            x_copy(kind, dx, d).start()

    def kv_block(kind, d, cc):
        return kv.at[kind, cc * NY + (y + d + NY) % NY]

    def y_gather(kind):
        ref = kv_block(kind, 0, core)
        if NC == 2:
            core_copy(kind, 0).start()
        for d in y_order[1:]:
            remote(ref, ref, kv_send.at[kind, d], kv_recv.at[kind, d], at_y(d)).start()

    def core_copy(kind, d):
        ref = kv_block(kind, d, core)
        return remote(ref, ref, ks_send.at[kind, d], ks_recv.at[kind, d], sibling)

    def y_arrived(kind, d):
        ref = kv_block(kind, d, core)
        back = (NY - d) % NY
        remote(ref, ref, kv_send.at[kind, back], kv_recv.at[kind, back], at_y(1)).wait_recv()
        if NC == 2:
            core_copy(kind, d).start()

    def core_arrived(kind, d):
        ref = kv_block(kind, d, NC - 1 - core)
        remote(ref, ref, ks_send.at[kind, d], ks_recv.at[kind, d], sibling).wait_recv()

    for kind in (0, 2, 1, 3):
        for d in z_order[1:]:
            a_copy(kind, d).start()
    local[2].wait()
    x_piece(0, 0)

    row_in = lax.broadcasted_iota(jnp.int32, (ROWS, HD), 0)
    for cc in range(NC):
        for yy in range(NY):
            for zz in range(NZ):
                base = order[(yy // 2) * (NZ * NC) + zz * NC + cc] * 128 + ((yy % 2) * NX + x) * ROWS
                pos_u[cc * NY + yy, pl.ds(zz * ROWS, ROWS), :] = row_in + base
    t_lane = lax.broadcasted_iota(jnp.int32, (8, T), 1)
    row_pos = jnp.zeros((8, T), jnp.int32)
    for zz in range(NZ):
        base = order[yh * (NZ * NC) + zz * NC + core] * 128 + yl * NX * ROWS
        row_pos = jnp.where(t_lane // ROWS == zz, base + t_lane % ROWS, row_pos)
    pos_t[...] = row_pos

    local[0].wait()
    local[1].wait()
    lane = lax.broadcasted_iota(jnp.int32, (ROWS, HD), 1)

    def rowdots(zz, carry):
        spread = jnp.zeros((ROWS, HD), F32)
        for h in range(GROUP):
            cols = pl.ds(pl.multiple_of(zz * W + h * HD, HD), HD)
            dots = jnp.sum(g_buf[:, cols].astype(F32) * o_buf[:, cols].astype(F32), axis=1, keepdims=True)
            spread = jnp.where(lane // 32 == h, dots, spread)
        high = spread.astype(BF16).astype(F32)
        rest = spread - high
        middle = rest.astype(BF16).astype(F32)
        low = rest - middle
        piece = lane % 32
        pieces = jnp.where(piece == 0, high, jnp.where(piece == 1, middle, jnp.where(piece == 2, low, 0.0)))
        r_buf[zz] = pieces.astype(BF16)
        return carry

    lax.fori_loop(0, NZ, rowdots, 0)
    r_own[zrow(z), :] = r_buf[z]
    for d in z_order[1:]:
        a_copy(4, d).start()
    for copy in local[3:]:
        copy.wait()

    for d in z_order[1:3]:
        x_piece(0, d)
    for d in z_order[1:]:
        a_arrived(0, d)
    y_gather(0)
    for d in z_order[3:]:
        x_piece(0, d)
    for d in z_order[1:]:
        a_arrived(1, d)
    y_gather(1)

    scale = INV_ROOT * LOG2E

    def key_rows(which, j):
        return kv[which, pl.ds(2 * j, 2)].reshape(2 * T, HD)

    def side_by_side(kind, xs):
        return jnp.concatenate([qg[kind, xs, :, h * HD:(h + 1) * HD].T for h in range(GROUP)], axis=1)

    def stacked(kind, xs):
        return jnp.concatenate([qg[kind, xs, :, h * HD:(h + 1) * HD] for h in range(GROUP)], axis=0)

    def score_tile(j, xs):
        s = dot_nn(key_rows(0, j), qt_buf[xs])
        seen = pos_u[pl.ds(2 * j, 2)].reshape(2 * T, HD)[:, :T] <= pos_t[0:1, :] + xs * ROWS
        for h in range(GROUP):
            cols = slice(h * T, (h + 1) * T)
            part = jnp.where(seen, s[:, cols] * scale, NEG)
            top = jnp.max(part, axis=0, keepdims=True)
            e = jnp.exp2(part - top)
            e_buf[j, xs, :, cols] = e
            m_buf[j, xs, :, cols] = top
            l_buf[j, xs, :, cols] = jnp.sum(e, axis=0, keepdims=True)

    def score_chunk(j):
        for xs in range(NX):
            score_tile(j, xs)

    mate = (1 - 2 * yl + NY) % NY
    near_tiles = [(cc, dx) for cc in range(NC) for dx in (0, 1, 3, 2)]
    per_piece = len(near_tiles) // NZ
    for i, d in enumerate(z_order):
        x_piece(1, d)
        for cc, dx in near_tiles[i * per_piece:(i + 1) * per_piece]:
            xs = (x + NX - dx) % NX
            if cc == 0:
                if dx == 0:
                    y_arrived(0, mate)
                else:
                    for dd in z_order:
                        x_arrived(0, dx, dd)
                qt_buf[xs] = side_by_side(0, xs)
            elif dx == 0:
                core_arrived(0, 0)
                core_arrived(0, mate)
            score_tile(((core + cc) % NC) * NP + yh, xs)

    for d in z_order[1:]:
        a_arrived(4, d)
    pick_row = lax.broadcasted_iota(jnp.int32, (8, HD), 0)
    pick_lane = lax.broadcasted_iota(jnp.int32, (8, HD), 1)
    pick = jnp.where((pick_lane // 32 == pick_row) & (pick_lane % 32 < 3), 1.0, 0.0).astype(BF16)
    rd_buf[x] = dot_nt(pick, r_own[...])

    def rd_copy(d):
        return remote(rd_buf.at[x], rd_buf.at[x], rd_send.at[d], rd_recv.at[d], at_x(d))

    for d in range(1, NX):
        rd_copy(d).start()

    def pair_offsets(p):
        return [(2 * p + e - y + 2 * NY) % NY for e in (0, 1)]

    def near_pair(i):
        rel = i + i // 2 - 2 * (i // 3) if NP == 4 else i
        return (yh + rel) % NP

    def scores_of(p, both, from_sibling):
        for d in both:
            y_arrived(0, d)
        score_chunk(core * NP + p)
        if NC == 2:
            for d in from_sibling:
                core_arrived(0, d)
            score_chunk((NC - 1 - core) * NP + p)

    def scores_far(i, carry):
        p = near_pair(i)
        scores_of(p, pair_offsets(p), pair_offsets(p))
        return carry

    lax.fori_loop(1, NP, scores_far, 0)
    for xs in range(NX):
        top = m_buf[0, xs]
        for j in range(1, NJ):
            top = jnp.maximum(top, m_buf[j, xs])
        total = l_buf[0, xs] * jnp.exp2(m_buf[0, xs] - top)
        for j in range(1, NJ):
            total = total + l_buf[j, xs] * jnp.exp2(m_buf[j, xs] - top)
        st[x, xs, 0:1, :] = top
        st[x, xs, 1:2, :] = total

    def st_copy(d):
        return remote(st.at[x], st.at[x], st_send.at[d], st_recv.at[d], at_x(d))

    for d in range(1, NX):
        st_copy(d).start()

    for dx in range(1, NX):
        for d in z_order:
            x_arrived(1, dx, d)
    for xs in range(NX):
        gt_buf[xs] = side_by_side(1, xs)
    for d in range(1, NX):
        ref = rd_buf.at[(x + NX - d) % NX]
        remote(ref, ref, rd_send.at[d], rd_recv.at[d], at_x(d)).wait_recv()
    for b in range(NC * NY):
        kt_buf[:, b * T:(b + 1) * T] = kv[0, b].T

    def dprobs_chunk(j):
        for xs in range(NX):
            rowdot = jnp.concatenate([rd_buf[xs, h:h + 1, :] for h in range(GROUP)], axis=1)
            dp_buf[j, xs] = dot_nn(key_rows(1, j), gt_buf[xs]) - rowdot

    def dprobs_of(p, both, from_sibling):
        for d in both:
            y_arrived(1, d)
        dprobs_chunk(core * NP + p)
        if NC == 2:
            for d in from_sibling:
                core_arrived(1, d)
            dprobs_chunk((NC - 1 - core) * NP + p)

    def dprobs_far(i, carry):
        p = near_pair(i)
        dprobs_of(p, pair_offsets(p), pair_offsets(p))
        return carry

    dprobs_of(yh, [mate], [0, mate])
    lax.fori_loop(1, NP, dprobs_far, 0)
    for d in range(1, NX):
        ref = st.at[(x + NX - d) % NX]
        remote(ref, ref, st_send.at[d], st_recv.at[d], at_x(d)).wait_recv()
    for xs in range(NX):
        top = st[0, xs, 0:1, :]
        for other in range(1, NX):
            top = jnp.maximum(top, st[other, xs, 0:1, :])
        total = jnp.zeros((1, GROUP * T), F32)
        for other in range(NX):
            total = total + st[other, xs, 1:2, :] * jnp.exp2(st[other, xs, 0:1, :] - top)
        lse[xs] = top + jnp.log2(total)

    for j in range(NJ):
        for xs in range(NX):
            m_buf[j, xs] = jnp.exp2(m_buf[j, xs] - lse[xs])

    def sib_copy(kind, p):
        return remote(sib_send.at[kind, p], sib_recv.at[kind, p], sb_send.at[kind, p], sb_recv.at[kind, p], sibling)

    def y_copy(kind, p, half_of):
        d = (2 * p + half_of - y + 2 * NY) % NY
        src = y_send.at[kind, p, pl.ds(pl.multiple_of(half_of * T, T), T), :]
        return remote(src, y_recv.at[kind, d], yd_send.at[kind, d], yd_recv.at[kind, d], at_y(d))

    def key_chunk(j):
        part = jnp.zeros((2 * T, HD), F32)
        for xs in range(NX):
            ds = (e_buf[j, xs] * m_buf[j, xs] * dp_buf[j, xs]).astype(BF16)
            ds_buf[xs, j] = ds
            part = part + dot_nn(ds, stacked(0, xs))
        return part

    def value_chunk(j):
        part = jnp.zeros((2 * T, HD), F32)
        for xs in range(NX):
            part = part + dot_nn((e_buf[j, xs] * m_buf[j, xs]).astype(BF16), stacked(1, xs))
        return part

    def both_cores(kind, chunk, p):
        if NC == 2:
            sib_send[kind, p] = chunk((NC - 1 - core) * NP + p).astype(BF16)
            sib_copy(kind, p).start()
        part = chunk(core * NP + p)
        if NC == 2:
            sib_copy(kind, p).wait_recv()
            part = part + sib_recv[kind, p].astype(F32)
        y_send[kind, p] = part.astype(BF16)
        return part

    def all_pairs(kind, chunk):
        def far_pair(i, carry):
            p = near_pair(NP - 1 - i)
            both_cores(kind, chunk, p)
            y_copy(kind, p, 0).start()
            y_copy(kind, p, 1).start()
            return carry

        lax.fori_loop(0, NP - 1, far_pair, 0)
        own_dkv[kind] = both_cores(kind, chunk, yh)
        y_copy(kind, yh, 1 - yl).start()

    all_pairs(0, key_chunk)

    def dq_copy(d):
        to = (x + d) % NX
        return remote(dq_send.at[to], dq_recv.at[d], xd_send.at[d], xd_recv.at[d], at_x(d))

    def query_block(xs):
        return dot_nn(kt_buf[...], ds_buf[xs].reshape(NJ * 2 * T, GROUP * T))

    for d in (2, 1, 3):
        to = (x + d) % NX
        dq_send[to] = query_block(to).astype(BF16)
        dq_copy(d).start()
    dq_own[...] = query_block(x)

    all_pairs(1, value_chunk)

    def out_copy(kind, d):
        to = (z + d) % NZ
        src, dst = {
            0: (dq_fin.at[zrow(to), :], q_out.at[:, zcol(z, W)]),
            1: (dkv_fin.at[0, zrow(to), :], k_out.at[:, zcol(z, HD)]),
            2: (dkv_fin.at[1, zrow(to), :], v_out.at[:, zcol(z, HD)]),
        }[kind]
        if d == 0:
            return pltpu.make_async_copy(src, dst, zo_send.at[kind, 0])
        return remote(src, dst, zo_send.at[kind, d], zo_recv.at[kind, d], at_z(d))

    own_rows = pl.ds(pl.multiple_of(yl * T, T), T)

    dq = dq_own[...]
    for d in range(1, NX):
        ref = dq_recv.at[d]
        remote(ref, ref, xd_send.at[d], xd_recv.at[d], at_x(d)).wait_recv()
        dq = dq + dq_recv[d].astype(F32)
    dq = dq * INV_ROOT
    for h in range(GROUP):
        dq_fin[:, h * HD:(h + 1) * HD] = dq[:, h * T:(h + 1) * T].T.astype(BF16)
    for d in z_order:
        out_copy(0, d).start()
    for kind, factor in ((0, INV_ROOT), (1, 1.0)):
        total = own_dkv[kind, own_rows, :]
        for d in range(1, NY):
            ref = y_recv.at[kind, d]
            remote(ref, ref, yd_send.at[kind, d], yd_recv.at[kind, d], at_y(d)).wait_recv()
            total = total + y_recv[kind, d].astype(F32)
        dkv_fin[kind] = (total * factor).astype(BF16)
        for d in z_order:
            out_copy(1 + kind, d).start()

    for kind in range(3):
        out_copy(kind, 0).wait()
    for d in z_order[1:]:
        src = (z + NZ - d) % NZ
        for kind, ref in (
            (0, q_out.at[:, zcol(src, W)]),
            (1, k_out.at[:, zcol(src, HD)]),
            (2, v_out.at[:, zcol(src, HD)]),
        ):
            remote(ref, ref, zo_send.at[kind, d], zo_recv.at[kind, d], at_z(d)).wait_recv()
    for d in z_order[1:]:
        for kind in range(5):
            a_copy(kind, d).wait_send()
        for kind in range(3):
            out_copy(kind, d).wait_send()
    for d in range(NZ):
        for dx in range(1, NX):
            x_copy(0, dx, d).wait_send()
            x_copy(1, dx, d).wait_send()
    for kind in (0, 1):
        ref = kv_block(kind, 0, core)
        for d in range(1, NY):
            remote(ref, ref, kv_send.at[kind, d], kv_recv.at[kind, d], at_y(d)).wait_send()
        if NC == 2:
            for d in range(NY):
                core_copy(kind, d).wait_send()
    if NC == 2:
        for p in range(NP):
            sib_copy(0, p).wait_send()
            sib_copy(1, p).wait_send()
    for d in range(1, NX):
        rd_copy(d).wait_send()
        st_copy(d).wait_send()
        dq_copy(d).wait_send()
    for d in range(1, NY):
        for kind in (0, 1):
            ref = y_recv.at[kind, d]
            remote(ref, ref, yd_send.at[kind, d], yd_recv.at[kind, d], at_y(d)).wait_send()


def copy_kernel(q_from, k_from, v_from, q_to, k_to, v_to, sem):
    copies = [
        pltpu.make_async_copy(q_from, q_to, sem.at[0]),
        pltpu.make_async_copy(k_from, k_to, sem.at[1]),
        pltpu.make_async_copy(v_from, v_to, sem.at[2]),
    ]
    for copy in copies:
        copy.start()
    for copy in copies:
        copy.wait()


def on_device(queries, keys, values, outputs, grad_out, span_order):
    T = NZ * ROWS
    NJ = NC * NY // 2
    NP = NY // 2
    vmem = pltpu.VMEM
    dma = pltpu.SemaphoreType.DMA
    width = W * NZ
    kv_width = HD * NZ
    scratch = [
        vmem((ROWS, width), BF16),
        vmem((ROWS, width), BF16),
        vmem((NZ, ROWS, HD), BF16),
        vmem((T, HD), BF16),
        vmem((NX, 8, T), F32),
        vmem((2, NX, T, W), BF16),
        vmem((2, NC * NY, T, HD), BF16),
        vmem((NC * NY, T, HD), jnp.int32),
        vmem((8, T), jnp.int32),
        vmem((NX, HD, GROUP * T), BF16),
        vmem((NX, HD, GROUP * T), BF16),
        vmem((HD, NC * NY * T), BF16),
        vmem((NJ, NX, 2 * T, GROUP * T), F32),
        vmem((NJ, NX, 2 * T, GROUP * T), F32),
        vmem((NX, NJ, 2 * T, GROUP * T), BF16),
        vmem((NJ, NX, 1, GROUP * T), F32),
        vmem((NJ, NX, 1, GROUP * T), F32),
        vmem((NX, NX, 2, GROUP * T), F32),
        vmem((NX, 1, GROUP * T), F32),
        vmem((HD, GROUP * T), F32),
        vmem((NX, HD, GROUP * T), BF16),
        vmem((NX, HD, GROUP * T), BF16),
        vmem((2, NP, 2 * T, HD), BF16),
        vmem((2, NP, 2 * T, HD), BF16),
        vmem((2, NP, 2 * T, HD), BF16),
        vmem((2, NY, T, HD), BF16),
        vmem((2, 2 * T, HD), F32),
        vmem((T, W), BF16),
        vmem((2, T, HD), BF16),
        dma((6,)),
        dma((5, NZ)), dma((5, NZ)),
        dma((2, NX, NZ)), dma((2, NX, NZ)),
        dma((NX,)), dma((NX,)),
        dma((2, NY)), dma((2, NY)),
        dma((2, NY)), dma((2, NY)),
        dma((NX,)), dma((NX,)),
        dma((2, NP)), dma((2, NP)),
        dma((2, NY)), dma((2, NY)),
        dma((NX,)), dma((NX,)),
        dma((3, NZ)), dma((3, NZ)),
    ]
    anywhere = pl.BlockSpec(memory_space=pl.ANY)
    in_vmem = pl.BlockSpec(memory_space=pltpu.VMEM)
    shapes = (
        jax.ShapeDtypeStruct((ROWS, width), BF16),
        jax.ShapeDtypeStruct((ROWS, kv_width), BF16),
        jax.ShapeDtypeStruct((ROWS, kv_width), BF16),
    )
    grads = pl.pallas_call(
        kernel,
        out_shape=shapes,
        in_specs=[anywhere] * 5 + [pl.BlockSpec(memory_space=pltpu.SMEM)],
        out_specs=(in_vmem, in_vmem, in_vmem),
        scratch_shapes=scratch,
        compiler_params=pltpu.CompilerParams(
            collective_id=0, has_side_effects=True, vmem_limit_bytes=56 * 1024 * 1024
        ),
    )(queries, keys, values, outputs, grad_out, span_order)
    return pl.pallas_call(
        copy_kernel,
        out_shape=shapes,
        in_specs=[in_vmem, in_vmem, in_vmem],
        out_specs=(anywhere, anywhere, anywhere),
        scratch_shapes=[dma((3,))],
    )(*grads)


def solution(mesh):
    rows = P(("blk", "head"), None)
    return jax.shard_map(
        on_device,
        mesh=mesh,
        in_specs=(rows, rows, rows, rows, rows, P()),
        out_specs=(rows, rows, rows),
        check_vma=False,
    )
```

```python
import math

import jax
import jax.numpy as jnp
from jax import lax
from jax.experimental import pallas as pl
from jax.experimental.pallas import tpu as pltpu
from jax.sharding import PartitionSpec as P

NX, NY, NZ, NC = 4, 8, 8, 2
ROWS = 16
HD = 128
GROUP = 4
W = GROUP * HD
NEG = -1e30
MESH = pl.DeviceIdType.MESH
F32 = jnp.float32
BF16 = jnp.bfloat16
INV_ROOT = 1.0 / math.sqrt(HD)
LOG2E = 1.4426950408889634


def near_first(n):
    order = [0]
    for step in range(1, n):
        if step not in order:
            order.append(step)
        if n - step not in order and n - step > 0:
            order.append(n - step)
    return order


def dot_nt(a, b):
    return lax.dot_general(a, b, (((1,), (1,)), ((), ())), preferred_element_type=F32)


def dot_nn(a, b):
    return lax.dot_general(a, b, (((1,), (0,)), ((), ())), preferred_element_type=F32)


def dot_tn(a, b):
    return lax.dot_general(a, b, (((0,), (0,)), ((), ())), preferred_element_type=F32)


def kernel(
    q_in, k_in, v_in, o_in, g_in, order,
    q_out, k_out, v_out,
    o_buf, g_buf, r_buf, r_own, rd_buf, qg, kv, pos_u, pos_t, qt_buf, gt_buf, kt_buf, e_buf, dp_buf, ds_buf, m_buf, l_buf, st, lse,
    dq_own, dq_send, dq_recv, sib_send, sib_recv, y_send, y_recv, own_dkv, dq_fin, dkv_fin,
    loc_sem, a_send, a_recv, x_send, x_recv, rd_send, rd_recv, kv_send, kv_recv,
    ks_send, ks_recv, st_send, st_recv, sb_send, sb_recv, yd_send, yd_recv, xd_send, xd_recv, zo_send, zo_recv, zl_sem,
):
    T = NZ * ROWS
    NJ = NC * NY // 2
    NP = NY // 2
    blk = lax.axis_index("blk")
    sub = lax.axis_index("head")
    core = blk % NC
    z = (blk // NC) % NZ
    yh = blk // (NC * NZ)
    x = sub % NX
    yl = sub // NX
    y = yh * 2 + yl
    slot = core * NY + y

    def dev(xx, yy, zz, cc):
        return ((yy // 2) * (NZ * NC) + zz * NC + cc, (yy % 2) * NX + xx)

    def at_x(d):
        return dev((x + d) % NX, y, z, core)

    def at_y(d):
        return dev(x, (y + d) % NY, z, core)

    def at_z(d):
        return dev(x, y, (z + d) % NZ, core)

    sibling = dev(x, y, z, (core + 1) % NC)

    def remote(src, dst, send_sem, recv_sem, who):
        return pltpu.make_async_remote_copy(
            src_ref=src, dst_ref=dst, send_sem=send_sem, recv_sem=recv_sem, device_id=who, device_id_type=MESH
        )

    def zrow(index):
        return pl.ds(pl.multiple_of(index * ROWS, ROWS), ROWS)

    def zcol(index, width):
        return pl.ds(pl.multiple_of(index * width, width), width)

    barrier = pltpu.get_barrier_semaphore()
    peers = [at_z(d) for d in near_first(NZ)[:0:-1]] + [at_y(d) for d in near_first(NY)[:0:-1]]
    peers += [at_x(d) for d in range(1, NX)]
    if NC == 2:
        peers.append(sibling)
    for who in peers:
        pl.semaphore_signal(barrier, inc=1, device_id=who, device_id_type=MESH)

    local = [
        pltpu.make_async_copy(o_in, o_buf, loc_sem.at[0]),
        pltpu.make_async_copy(g_in, g_buf, loc_sem.at[1]),
        pltpu.make_async_copy(q_in.at[:, zcol(z, W)], qg.at[0, x, zrow(z), :], loc_sem.at[2]),
        pltpu.make_async_copy(g_in.at[:, zcol(z, W)], qg.at[1, x, zrow(z), :], loc_sem.at[3]),
        pltpu.make_async_copy(k_in.at[:, zcol(z, HD)], kv.at[0, slot, zrow(z), :], loc_sem.at[4]),
        pltpu.make_async_copy(v_in.at[:, zcol(z, HD)], kv.at[1, slot, zrow(z), :], loc_sem.at[5]),
    ]
    for copy in local:
        copy.start()

    pl.semaphore_wait(barrier, len(peers))

    z_order = near_first(NZ)
    y_order = near_first(NY)

    def a_copy(kind, d):
        to = (z + d) % NZ
        src, dst = {
            0: (k_in.at[:, zcol(to, HD)], kv.at[0, slot, zrow(z), :]),
            1: (v_in.at[:, zcol(to, HD)], kv.at[1, slot, zrow(z), :]),
            2: (q_in.at[:, zcol(to, W)], qg.at[0, x, zrow(z), :]),
            3: (g_in.at[:, zcol(to, W)], qg.at[1, x, zrow(z), :]),
            4: (r_buf.at[to], r_own.at[zrow(z), :]),
        }[kind]
        return remote(src, dst, a_send.at[kind], a_recv.at[kind, d], at_z(d))

    def a_arrived(kind, d):
        row = zrow((z + NZ - d) % NZ)
        ref = {
            0: kv.at[0, slot, row, :],
            1: kv.at[1, slot, row, :],
            2: qg.at[0, x, row, :],
            3: qg.at[1, x, row, :],
            4: r_own.at[row, :],
        }[kind]
        remote(ref, ref, a_send.at[kind], a_recv.at[kind, d], at_z(d)).wait_recv()

    def x_copy(kind, dx, d):
        ref = qg.at[kind, x, zrow((z + NZ - d) % NZ), :]
        return remote(ref, ref, x_send.at[kind, dx], x_recv.at[kind, dx], at_x(dx))

    def x_whole(kind, dx):
        ref = qg.at[kind, (x + NX - dx) % NX]
        return remote(ref, ref, x_send.at[kind, dx], x_recv.at[kind, dx], at_x(dx))

    def x_piece(kind, d):
        if d > 0:
            a_arrived(2 + kind, d)
        for dx in (2, 1, 3):
            x_copy(kind, dx, d).start()

    def kv_block(kind, d, cc):
        return kv.at[kind, cc * NY + (y + d + NY) % NY]

    def y_gather(kind):
        ref = kv_block(kind, 0, core)
        if NC == 2:
            core_copy(kind, 0).start()
        for d in y_order[1:]:
            remote(ref, ref, kv_send.at[kind, d], kv_recv.at[kind, d], at_y(d)).start()

    def core_copy(kind, d):
        ref = kv_block(kind, d, core)
        return remote(ref, ref, ks_send.at[kind, d], ks_recv.at[kind, d], sibling)

    def y_arrived(kind, d):
        ref = kv_block(kind, d, core)
        back = (NY - d) % NY
        remote(ref, ref, kv_send.at[kind, back], kv_recv.at[kind, back], at_y(1)).wait_recv()
        if NC == 2:
            core_copy(kind, d).start()

    def core_arrived(kind, d):
        ref = kv_block(kind, d, NC - 1 - core)
        remote(ref, ref, ks_send.at[kind, d], ks_recv.at[kind, d], sibling).wait_recv()

    for kind in (0, 2, 1, 3):
        for d in z_order[1:]:
            a_copy(kind, d).start()
    local[2].wait()
    x_piece(0, 0)

    row_in = lax.broadcasted_iota(jnp.int32, (ROWS, HD), 0)
    for cc in range(NC):
        for yy in range(NY):
            for zz in range(NZ):
                base = order[(yy // 2) * (NZ * NC) + zz * NC + cc] * 128 + ((yy % 2) * NX + x) * ROWS
                pos_u[cc * NY + yy, pl.ds(zz * ROWS, ROWS), :] = row_in + base
    t_lane = lax.broadcasted_iota(jnp.int32, (8, T), 1)
    row_pos = jnp.zeros((8, T), jnp.int32)
    for zz in range(NZ):
        base = order[yh * (NZ * NC) + zz * NC + core] * 128 + yl * NX * ROWS
        row_pos = jnp.where(t_lane // ROWS == zz, base + t_lane % ROWS, row_pos)
    pos_t[...] = row_pos

    local[0].wait()
    local[1].wait()
    lane = lax.broadcasted_iota(jnp.int32, (ROWS, HD), 1)

    def rowdots(zz, carry):
        spread = jnp.zeros((ROWS, HD), F32)
        for h in range(GROUP):
            cols = pl.ds(pl.multiple_of(zz * W + h * HD, HD), HD)
            dots = jnp.sum(g_buf[:, cols].astype(F32) * o_buf[:, cols].astype(F32), axis=1, keepdims=True)
            spread = jnp.where(lane // 32 == h, dots, spread)
        high = spread.astype(BF16).astype(F32)
        rest = spread - high
        middle = rest.astype(BF16).astype(F32)
        low = rest - middle
        piece = lane % 32
        pieces = jnp.where(piece == 0, high, jnp.where(piece == 1, middle, jnp.where(piece == 2, low, 0.0)))
        r_buf[zz] = pieces.astype(BF16)
        return carry

    lax.fori_loop(0, NZ, rowdots, 0)
    r_own[zrow(z), :] = r_buf[z]
    for d in z_order[1:]:
        a_copy(4, d).start()
    for copy in local[3:]:
        copy.wait()

    for d in z_order[1:3]:
        x_piece(0, d)
    for d in z_order[1:]:
        a_arrived(0, d)
    y_gather(0)
    for d in z_order[3:]:
        x_piece(0, d)
    for d in z_order[1:]:
        a_arrived(1, d)
    y_gather(1)

    scale = INV_ROOT * LOG2E

    def key_rows(which, j):
        return kv[which, pl.ds(2 * j, 2)].reshape(2 * T, HD)

    def side_by_side(kind, xs):
        return jnp.concatenate([qg[kind, xs, :, h * HD:(h + 1) * HD].T for h in range(GROUP)], axis=1)

    def stacked(kind, xs):
        return jnp.concatenate([qg[kind, xs, :, h * HD:(h + 1) * HD] for h in range(GROUP)], axis=0)

    def score_tile(j, xs):
        s = dot_nn(key_rows(0, j), qt_buf[xs])
        seen = pos_u[pl.ds(2 * j, 2)].reshape(2 * T, HD)[:, :T] <= pos_t[0:1, :] + xs * ROWS
        for h in range(GROUP):
            cols = slice(h * T, (h + 1) * T)
            part = jnp.where(seen, s[:, cols] * scale, NEG)
            top = jnp.max(part, axis=0, keepdims=True)
            e = jnp.exp2(part - top)
            e_buf[j, xs, :, cols] = e
            m_buf[j, xs, :, cols] = top
            l_buf[j, xs, :, cols] = jnp.sum(e, axis=0, keepdims=True)

    def score_chunk(j):
        for xs in range(NX):
            score_tile(j, xs)

    mate = (1 - 2 * yl + NY) % NY
    near_tiles = [(cc, dx) for cc in range(NC) for dx in (0, 1, 3, 2)]
    per_piece = len(near_tiles) // NZ
    for i, d in enumerate(z_order):
        x_piece(1, d)
        for cc, dx in near_tiles[i * per_piece:(i + 1) * per_piece]:
            xs = (x + NX - dx) % NX
            if cc == 0:
                if dx == 0:
                    y_arrived(0, mate)
                else:
                    x_whole(0, dx).wait_recv()
                qt_buf[xs] = side_by_side(0, xs)
            elif dx == 0:
                core_arrived(0, 0)
                core_arrived(0, mate)
            score_tile(((core + cc) % NC) * NP + yh, xs)

    for d in z_order[1:]:
        a_arrived(4, d)
    pick_row = lax.broadcasted_iota(jnp.int32, (8, HD), 0)
    pick_lane = lax.broadcasted_iota(jnp.int32, (8, HD), 1)
    pick = jnp.where((pick_lane // 32 == pick_row) & (pick_lane % 32 < 3), 1.0, 0.0).astype(BF16)
    rd_buf[x] = dot_nt(pick, r_own[...])

    def rd_copy(d):
        return remote(rd_buf.at[x], rd_buf.at[x], rd_send.at[d], rd_recv.at[d], at_x(d))

    for d in range(1, NX):
        rd_copy(d).start()

    def pair_offsets(p):
        return [(2 * p + e - y + 2 * NY) % NY for e in (0, 1)]

    def near_pair(i):
        rel = i + i // 2 - 2 * (i // 3) if NP == 4 else i
        return (yh + rel) % NP

    def own_blocks(kind, chunk, i):
        p = near_pair(i)
        for d in pair_offsets(p):
            y_arrived(kind, d)
        chunk(core * NP + p)

    def other_blocks(kind, chunk, i):
        if NC == 2:
            p = near_pair(i)
            for d in pair_offsets(p):
                core_arrived(kind, d)
            chunk((NC - 1 - core) * NP + p)

    def skewed(kind, chunk):
        def body(i, carry):
            own_blocks(kind, chunk, i)
            other_blocks(kind, chunk, i - 1)
            return carry

        return body

    if NP > 1:
        own_blocks(0, score_chunk, 1)
        lax.fori_loop(2, NP, skewed(0, score_chunk), 0)
        other_blocks(0, score_chunk, NP - 1)
    for xs in range(NX):
        top = m_buf[0, xs]
        for j in range(1, NJ):
            top = jnp.maximum(top, m_buf[j, xs])
        total = l_buf[0, xs] * jnp.exp2(m_buf[0, xs] - top)
        for j in range(1, NJ):
            total = total + l_buf[j, xs] * jnp.exp2(m_buf[j, xs] - top)
        st[x, xs, 0:1, :] = top
        st[x, xs, 1:2, :] = total

    def st_copy(d):
        return remote(st.at[x], st.at[x], st_send.at[d], st_recv.at[d], at_x(d))

    for d in range(1, NX):
        st_copy(d).start()

    for dx in range(1, NX):
        x_whole(1, dx).wait_recv()
    for xs in range(NX):
        gt_buf[xs] = side_by_side(1, xs)
    for d in range(1, NX):
        ref = rd_buf.at[(x + NX - d) % NX]
        remote(ref, ref, rd_send.at[d], rd_recv.at[d], at_x(d)).wait_recv()
    for b in range(NC * NY):
        kt_buf[:, b * T:(b + 1) * T] = kv[0, b].T

    def dprobs_chunk(j):
        for xs in range(NX):
            rowdot = jnp.concatenate([rd_buf[xs, h:h + 1, :] for h in range(GROUP)], axis=1)
            dp_buf[j, xs] = dot_nn(key_rows(1, j), gt_buf[xs]) - rowdot

    y_arrived(1, mate)
    dprobs_chunk(core * NP + yh)
    lax.fori_loop(1, NP, skewed(1, dprobs_chunk), 0)
    other_blocks(1, dprobs_chunk, NP - 1)
    for d in range(1, NX):
        ref = st.at[(x + NX - d) % NX]
        remote(ref, ref, st_send.at[d], st_recv.at[d], at_x(d)).wait_recv()
    for xs in range(NX):
        top = st[0, xs, 0:1, :]
        for other in range(1, NX):
            top = jnp.maximum(top, st[other, xs, 0:1, :])
        total = jnp.zeros((1, GROUP * T), F32)
        for other in range(NX):
            total = total + st[other, xs, 1:2, :] * jnp.exp2(st[other, xs, 0:1, :] - top)
        lse[xs] = top + jnp.log2(total)

    for j in range(NJ):
        for xs in range(NX):
            m_buf[j, xs] = jnp.exp2(m_buf[j, xs] - lse[xs])

    def sib_copy(kind, p):
        return remote(sib_send.at[kind, p], sib_recv.at[kind, p], sb_send.at[kind, p], sb_recv.at[kind, p], sibling)

    def y_copy(kind, p, half_of):
        d = (2 * p + half_of - y + 2 * NY) % NY
        src = y_send.at[kind, p, pl.ds(pl.multiple_of(half_of * T, T), T), :]
        return remote(src, y_recv.at[kind, d], yd_send.at[kind, d], yd_recv.at[kind, d], at_y(d))

    def key_chunk(j):
        part = jnp.zeros((2 * T, HD), F32)
        for xs in range(NX):
            ds = (e_buf[j, xs] * m_buf[j, xs] * dp_buf[j, xs]).astype(BF16)
            ds_buf[xs, j] = ds
            part = part + dot_nn(ds, stacked(0, xs))
        return part

    def value_chunk(j):
        part = jnp.zeros((2 * T, HD), F32)
        for xs in range(NX):
            part = part + dot_nn((e_buf[j, xs] * m_buf[j, xs]).astype(BF16), stacked(1, xs))
        return part

    def all_pairs(kind, chunk):
        def for_sibling(i, carry):
            p = near_pair(NP - 1 - i)
            sib_send[kind, p] = chunk((NC - 1 - core) * NP + p).astype(BF16)
            sib_copy(kind, p).start()
            return carry

        def own_pair(p):
            part = chunk(core * NP + p)
            if NC == 2:
                sib_copy(kind, p).wait_recv()
                part = part + sib_recv[kind, p].astype(F32)
            y_send[kind, p] = part.astype(BF16)
            return part

        def far_pair(i, carry):
            p = near_pair(NP - 1 - i)
            own_pair(p)
            y_copy(kind, p, 0).start()
            y_copy(kind, p, 1).start()
            return carry

        if NC == 2:
            lax.fori_loop(0, NP, for_sibling, 0)
        lax.fori_loop(0, NP - 1, far_pair, 0)
        own_dkv[kind] = own_pair(yh)
        y_copy(kind, yh, 1 - yl).start()

    all_pairs(0, key_chunk)

    def dq_copy(d):
        to = (x + d) % NX
        return remote(dq_send.at[to], dq_recv.at[d], xd_send.at[d], xd_recv.at[d], at_x(d))

    def query_block(xs):
        return dot_nn(kt_buf[...], ds_buf[xs].reshape(NJ * 2 * T, GROUP * T))

    for d in (2, 1, 3):
        to = (x + d) % NX
        dq_send[to] = query_block(to).astype(BF16)
        dq_copy(d).start()
    dq_own[...] = query_block(x)

    all_pairs(1, value_chunk)

    if NZ > 1:
        for kind, ref in enumerate((
            k_in.at[:, pl.ds(0, (NZ - 1) * HD)],
            v_in.at[:, pl.ds(0, (NZ - 1) * HD)],
            q_in.at[:, pl.ds(0, (NZ - 1) * W)],
            g_in.at[:, pl.ds(0, (NZ - 1) * W)],
            r_buf.at[pl.ds(0, NZ - 1)],
        )):
            remote(ref, ref, a_send.at[kind], a_recv.at[kind, 1], at_z(1)).wait_send()
    for kind in (0, 1):
        for dx in range(1, NX):
            x_whole(kind, dx).wait_send()
        ref = kv_block(kind, 0, core)
        for d in range(1, NY):
            remote(ref, ref, kv_send.at[kind, d], kv_recv.at[kind, d], at_y(d)).wait_send()
        if NC == 2:
            for d in range(NY):
                core_copy(kind, d).wait_send()
            for p in range(NP):
                sib_copy(kind, p).wait_send()
    for d in range(1, NX):
        rd_copy(d).wait_send()
        st_copy(d).wait_send()
        dq_copy(d).wait_send()

    def out_copy(kind, d):
        to = (z + d) % NZ
        src, dst = {
            0: (dq_fin.at[zrow(to), :], q_out.at[:, zcol(z, W)]),
            1: (dkv_fin.at[0, zrow(to), :], k_out.at[:, zcol(z, HD)]),
            2: (dkv_fin.at[1, zrow(to), :], v_out.at[:, zcol(z, HD)]),
        }[kind]
        if d == 0:
            return pltpu.make_async_copy(src, dst, zl_sem.at[kind])
        return remote(src, dst, zo_send.at[kind], zo_recv.at[kind], at_z(d))

    def out_whole(kind):
        ref = (q_out.at[:, pl.ds(0, (NZ - 1) * W)], k_out.at[:, pl.ds(0, (NZ - 1) * HD)], v_out.at[:, pl.ds(0, (NZ - 1) * HD)])[kind]
        return remote(ref, ref, zo_send.at[kind], zo_recv.at[kind], at_z(1))

    own_rows = pl.ds(pl.multiple_of(yl * T, T), T)

    dq = dq_own[...]
    for d in range(1, NX):
        ref = dq_recv.at[d]
        remote(ref, ref, xd_send.at[d], xd_recv.at[d], at_x(d)).wait_recv()
        dq = dq + dq_recv[d].astype(F32)
    dq = dq * INV_ROOT
    for h in range(GROUP):
        dq_fin[:, h * HD:(h + 1) * HD] = dq[:, h * T:(h + 1) * T].T.astype(BF16)
    for d in z_order:
        out_copy(0, d).start()
    for kind, factor in ((0, INV_ROOT), (1, 1.0)):
        total = own_dkv[kind, own_rows, :]
        for d in range(1, NY):
            ref = y_recv.at[kind, d]
            remote(ref, ref, yd_send.at[kind, d], yd_recv.at[kind, d], at_y(d)).wait_recv()
            total = total + y_recv[kind, d].astype(F32)
        dkv_fin[kind] = (total * factor).astype(BF16)
        for d in z_order:
            out_copy(1 + kind, d).start()

    for d in range(1, NY):
        for kind in (0, 1):
            ref = y_recv.at[kind, d]
            remote(ref, ref, yd_send.at[kind, d], yd_recv.at[kind, d], at_y(d)).wait_send()
    for kind in range(3):
        out_copy(kind, 0).wait()
        if NZ > 1:
            out_whole(kind).wait()


def copy_kernel(q_from, k_from, v_from, q_to, k_to, v_to, sem):
    copies = [
        pltpu.make_async_copy(q_from, q_to, sem.at[0]),
        pltpu.make_async_copy(k_from, k_to, sem.at[1]),
        pltpu.make_async_copy(v_from, v_to, sem.at[2]),
    ]
    for copy in copies:
        copy.start()
    for copy in copies:
        copy.wait()


def on_device(queries, keys, values, outputs, grad_out, span_order):
    T = NZ * ROWS
    NJ = NC * NY // 2
    NP = NY // 2
    vmem = pltpu.VMEM
    dma = pltpu.SemaphoreType.DMA
    width = W * NZ
    kv_width = HD * NZ
    scratch = [
        vmem((ROWS, width), BF16),
        vmem((ROWS, width), BF16),
        vmem((NZ, ROWS, HD), BF16),
        vmem((T, HD), BF16),
        vmem((NX, 8, T), F32),
        vmem((2, NX, T, W), BF16),
        vmem((2, NC * NY, T, HD), BF16),
        vmem((NC * NY, T, HD), jnp.int32),
        vmem((8, T), jnp.int32),
        vmem((NX, HD, GROUP * T), BF16),
        vmem((NX, HD, GROUP * T), BF16),
        vmem((HD, NC * NY * T), BF16),
        vmem((NJ, NX, 2 * T, GROUP * T), F32),
        vmem((NJ, NX, 2 * T, GROUP * T), F32),
        vmem((NX, NJ, 2 * T, GROUP * T), BF16),
        vmem((NJ, NX, 1, GROUP * T), F32),
        vmem((NJ, NX, 1, GROUP * T), F32),
        vmem((NX, NX, 2, GROUP * T), F32),
        vmem((NX, 1, GROUP * T), F32),
        vmem((HD, GROUP * T), F32),
        vmem((NX, HD, GROUP * T), BF16),
        vmem((NX, HD, GROUP * T), BF16),
        vmem((2, NP, 2 * T, HD), BF16),
        vmem((2, NP, 2 * T, HD), BF16),
        vmem((2, NP, 2 * T, HD), BF16),
        vmem((2, NY, T, HD), BF16),
        vmem((2, 2 * T, HD), F32),
        vmem((T, W), BF16),
        vmem((2, T, HD), BF16),
        dma((6,)),
        dma((5,)), dma((5, NZ)),
        dma((2, NX)), dma((2, NX)),
        dma((NX,)), dma((NX,)),
        dma((2, NY)), dma((2, NY)),
        dma((2, NY)), dma((2, NY)),
        dma((NX,)), dma((NX,)),
        dma((2, NP)), dma((2, NP)),
        dma((2, NY)), dma((2, NY)),
        dma((NX,)), dma((NX,)),
        dma((3,)), dma((3,)), dma((3,)),
    ]
    anywhere = pl.BlockSpec(memory_space=pl.ANY)
    in_vmem = pl.BlockSpec(memory_space=pltpu.VMEM)
    shapes = (
        jax.ShapeDtypeStruct((ROWS, width), BF16),
        jax.ShapeDtypeStruct((ROWS, kv_width), BF16),
        jax.ShapeDtypeStruct((ROWS, kv_width), BF16),
    )
    grads = pl.pallas_call(
        kernel,
        out_shape=shapes,
        in_specs=[anywhere] * 5 + [pl.BlockSpec(memory_space=pltpu.SMEM)],
        out_specs=(in_vmem, in_vmem, in_vmem),
        scratch_shapes=scratch,
        compiler_params=pltpu.CompilerParams(
            collective_id=0, has_side_effects=True, vmem_limit_bytes=56 * 1024 * 1024
        ),
    )(queries, keys, values, outputs, grad_out, span_order)
    return pl.pallas_call(
        copy_kernel,
        out_shape=shapes,
        in_specs=[in_vmem, in_vmem, in_vmem],
        out_specs=(anywhere, anywhere, anywhere),
        scratch_shapes=[dma((3,))],
    )(*grads)


def solution(mesh):
    rows = P(("blk", "head"), None)
    return jax.shard_map(
        on_device,
        mesh=mesh,
        in_specs=(rows, rows, rows, rows, rows, P()),
        out_specs=(rows, rows, rows),
        check_vma=False,
    )
```

```python
import math

import jax
import jax.numpy as jnp
from jax import lax
from jax.experimental import pallas as pl
from jax.experimental.pallas import tpu as pltpu
from jax.sharding import PartitionSpec as P

NX, NY, NZ, NC = 4, 8, 8, 2
ROWS = 16
HD = 128
GROUP = 4
W = GROUP * HD
NEG = -1e30
MESH = pl.DeviceIdType.MESH
F32 = jnp.float32
BF16 = jnp.bfloat16
INV_ROOT = 1.0 / math.sqrt(HD)
LOG2E = 1.4426950408889634


def near_first(n):
    order = [0]
    for step in range(1, n):
        if step not in order:
            order.append(step)
        if n - step not in order and n - step > 0:
            order.append(n - step)
    return order


def dot_nt(a, b):
    return lax.dot_general(a, b, (((1,), (1,)), ((), ())), preferred_element_type=F32)


def dot_nn(a, b):
    return lax.dot_general(a, b, (((1,), (0,)), ((), ())), preferred_element_type=F32)


def dot_tn(a, b):
    return lax.dot_general(a, b, (((0,), (0,)), ((), ())), preferred_element_type=F32)


def kernel(
    q_in, k_in, v_in, o_in, g_in, order,
    q_out, k_out, v_out,
    o_buf, g_buf, r_buf, r_own, rd_buf, qg, kv, pos_u, pos_t, qt_buf, gt_buf, kt_buf, e_buf, dp_buf, ds_buf, m_buf, l_buf, st, lse,
    dq_own, dq_send, dq_recv, sib_send, sib_recv, y_send, y_recv, own_dkv, dq_fin, dkv_fin,
    loc_sem, a_send, a_recv, x_send, x_recv, rd_send, rd_recv, kv_send, kv_recv,
    ks_send, ks_recv, st_send, st_recv, sb_send, sb_recv, yd_send, yd_recv, xd_send, xd_recv, zo_send, zo_recv, zl_sem,
):
    T = NZ * ROWS
    NJ = NC * NY // 2
    NP = NY // 2
    blk = lax.axis_index("blk")
    sub = lax.axis_index("head")
    core = blk % NC
    z = (blk // NC) % NZ
    yh = blk // (NC * NZ)
    x = sub % NX
    yl = sub // NX
    y = yh * 2 + yl
    slot = core * NY + y

    def dev(xx, yy, zz, cc):
        return ((yy // 2) * (NZ * NC) + zz * NC + cc, (yy % 2) * NX + xx)

    def at_x(d):
        return dev((x + d) % NX, y, z, core)

    def at_y(d):
        return dev(x, (y + d) % NY, z, core)

    def at_z(d):
        return dev(x, y, (z + d) % NZ, core)

    sibling = dev(x, y, z, (core + 1) % NC)

    def remote(src, dst, send_sem, recv_sem, who):
        return pltpu.make_async_remote_copy(
            src_ref=src, dst_ref=dst, send_sem=send_sem, recv_sem=recv_sem, device_id=who, device_id_type=MESH
        )

    def zrow(index):
        return pl.ds(pl.multiple_of(index * ROWS, ROWS), ROWS)

    def zcol(index, width):
        return pl.ds(pl.multiple_of(index * width, width), width)

    barrier = pltpu.get_barrier_semaphore()
    peers = [at_z(d) for d in near_first(NZ)[:0:-1]] + [at_y(d) for d in near_first(NY)[:0:-1]]
    peers += [at_x(d) for d in range(1, NX)]
    if NC == 2:
        peers.append(sibling)
    for who in peers:
        pl.semaphore_signal(barrier, inc=1, device_id=who, device_id_type=MESH)

    local = [
        pltpu.make_async_copy(o_in, o_buf, loc_sem.at[0]),
        pltpu.make_async_copy(g_in, g_buf, loc_sem.at[1]),
        pltpu.make_async_copy(q_in.at[:, zcol(z, W)], qg.at[0, x, zrow(z), :], loc_sem.at[2]),
        pltpu.make_async_copy(g_in.at[:, zcol(z, W)], qg.at[1, x, zrow(z), :], loc_sem.at[3]),
        pltpu.make_async_copy(k_in.at[:, zcol(z, HD)], kv.at[0, slot, zrow(z), :], loc_sem.at[4]),
        pltpu.make_async_copy(v_in.at[:, zcol(z, HD)], kv.at[1, slot, zrow(z), :], loc_sem.at[5]),
    ]
    for copy in local:
        copy.start()

    pl.semaphore_wait(barrier, len(peers))

    z_order = near_first(NZ)
    y_order = near_first(NY)
    mate = (1 - 2 * yl + NY) % NY

    def a_copy(kind, d):
        to = (z + d) % NZ
        src, dst = {
            0: (k_in.at[:, zcol(to, HD)], kv.at[0, slot, zrow(z), :]),
            1: (v_in.at[:, zcol(to, HD)], kv.at[1, slot, zrow(z), :]),
            2: (q_in.at[:, zcol(to, W)], qg.at[0, x, zrow(z), :]),
            3: (g_in.at[:, zcol(to, W)], qg.at[1, x, zrow(z), :]),
            4: (r_buf.at[to], r_own.at[zrow(z), :]),
        }[kind]
        return remote(src, dst, a_send.at[kind], a_recv.at[kind, d], at_z(d))

    def a_arrived(kind, d):
        row = zrow((z + NZ - d) % NZ)
        ref = {
            0: kv.at[0, slot, row, :],
            1: kv.at[1, slot, row, :],
            2: qg.at[0, x, row, :],
            3: qg.at[1, x, row, :],
            4: r_own.at[row, :],
        }[kind]
        remote(ref, ref, a_send.at[kind], a_recv.at[kind, d], at_z(d)).wait_recv()

    def x_copy(kind, dx, d):
        ref = qg.at[kind, x, zrow((z + NZ - d) % NZ), :]
        return remote(ref, ref, x_send.at[kind, dx], x_recv.at[kind, dx], at_x(dx))

    def x_whole(kind, dx):
        ref = qg.at[kind, (x + NX - dx) % NX]
        return remote(ref, ref, x_send.at[kind, dx], x_recv.at[kind, dx], at_x(dx))

    def x_piece(kind, d):
        if d > 0:
            a_arrived(2 + kind, d)
        for dx in (2, 1, 3):
            x_copy(kind, dx, d).start()

    def kv_block(kind, d, cc):
        return kv.at[kind, cc * NY + (y + d + NY) % NY]

    def y_gather(kind):
        ref = kv_block(kind, 0, core)
        if NC == 2:
            core_copy(kind, 0).start()
        for d in [mate] + y_order[:2:-1] + [NY - mate]:
            remote(ref, ref, kv_send.at[kind, d], kv_recv.at[kind, d], at_y(d)).start()

    def core_copy(kind, d):
        ref = kv_block(kind, d, core)
        return remote(ref, ref, ks_send.at[kind, d], ks_recv.at[kind, d], sibling)

    def y_arrived(kind, d):
        ref = kv_block(kind, d, core)
        back = (NY - d) % NY
        remote(ref, ref, kv_send.at[kind, back], kv_recv.at[kind, back], at_y(1)).wait_recv()
        if NC == 2:
            core_copy(kind, d).start()

    def core_arrived(kind, d):
        ref = kv_block(kind, d, NC - 1 - core)
        remote(ref, ref, ks_send.at[kind, d], ks_recv.at[kind, d], sibling).wait_recv()

    for kind in (0, 2, 1, 3):
        for d in z_order[1:]:
            a_copy(kind, d).start()
    local[2].wait()
    x_piece(0, 0)

    row_in = lax.broadcasted_iota(jnp.int32, (ROWS, HD), 0)
    for cc in range(NC):
        for yy in range(NY):
            for zz in range(NZ):
                base = order[(yy // 2) * (NZ * NC) + zz * NC + cc] * 128 + ((yy % 2) * NX + x) * ROWS
                pos_u[cc * NY + yy, pl.ds(zz * ROWS, ROWS), :] = row_in + base
    t_lane = lax.broadcasted_iota(jnp.int32, (8, T), 1)
    row_pos = jnp.zeros((8, T), jnp.int32)
    for zz in range(NZ):
        base = order[yh * (NZ * NC) + zz * NC + core] * 128 + yl * NX * ROWS
        row_pos = jnp.where(t_lane // ROWS == zz, base + t_lane % ROWS, row_pos)
    pos_t[...] = row_pos

    local[0].wait()
    local[1].wait()
    lane = lax.broadcasted_iota(jnp.int32, (ROWS, HD), 1)

    def rowdots(zz, carry):
        spread = jnp.zeros((ROWS, HD), F32)
        for h in range(GROUP):
            cols = pl.ds(pl.multiple_of(zz * W + h * HD, HD), HD)
            dots = jnp.sum(g_buf[:, cols].astype(F32) * o_buf[:, cols].astype(F32), axis=1, keepdims=True)
            spread = jnp.where(lane // 32 == h, dots, spread)
        high = spread.astype(BF16).astype(F32)
        rest = spread - high
        middle = rest.astype(BF16).astype(F32)
        low = rest - middle
        piece = lane % 32
        pieces = jnp.where(piece == 0, high, jnp.where(piece == 1, middle, jnp.where(piece == 2, low, 0.0)))
        r_buf[zz] = pieces.astype(BF16)
        return carry

    lax.fori_loop(0, NZ, rowdots, 0)
    r_own[zrow(z), :] = r_buf[z]
    for d in z_order[1:]:
        a_copy(4, d).start()
    for copy in local[3:]:
        copy.wait()

    for d in z_order[1:3]:
        x_piece(0, d)
    for d in z_order[1:]:
        a_arrived(0, d)
    y_gather(0)
    for d in z_order[3:]:
        x_piece(0, d)
    for d in z_order[1:]:
        a_arrived(1, d)
    y_gather(1)

    scale = INV_ROOT * LOG2E

    def key_rows(which, j):
        return kv[which, pl.ds(2 * j, 2)].reshape(2 * T, HD)

    def side_by_side(kind, xs):
        return jnp.concatenate([qg[kind, xs, :, h * HD:(h + 1) * HD].T for h in range(GROUP)], axis=1)

    def stacked(kind, xs):
        return jnp.concatenate([qg[kind, xs, :, h * HD:(h + 1) * HD] for h in range(GROUP)], axis=0)

    def score_tile(j, xs):
        s = dot_nn(key_rows(0, j), qt_buf[xs])
        seen = pos_u[pl.ds(2 * j, 2)].reshape(2 * T, HD)[:, :T] <= pos_t[0:1, :] + xs * ROWS
        for h in range(GROUP):
            cols = slice(h * T, (h + 1) * T)
            part = jnp.where(seen, s[:, cols] * scale, NEG)
            top = jnp.max(part, axis=0, keepdims=True)
            e = jnp.exp2(part - top)
            e_buf[j, xs, :, cols] = e
            m_buf[j, xs, :, cols] = top
            l_buf[j, xs, :, cols] = jnp.sum(e, axis=0, keepdims=True)

    def score_chunk(j):
        for xs in range(NX):
            score_tile(j, xs)

    near_tiles = [(cc, dx) for cc in range(NC) for dx in (0, 1, 3, 2)]
    per_piece = len(near_tiles) // NZ
    for i, d in enumerate(z_order):
        x_piece(1, d)
        for cc, dx in near_tiles[i * per_piece:(i + 1) * per_piece]:
            xs = (x + NX - dx) % NX
            if cc == 0:
                if dx == 0:
                    y_arrived(0, mate)
                else:
                    x_whole(0, dx).wait_recv()
                qt_buf[xs] = side_by_side(0, xs)
            elif dx == 0:
                core_arrived(0, 0)
                core_arrived(0, mate)
            score_tile(((core + cc) % NC) * NP + yh, xs)

    for d in z_order[1:]:
        a_arrived(4, d)
    pick_row = lax.broadcasted_iota(jnp.int32, (8, HD), 0)
    pick_lane = lax.broadcasted_iota(jnp.int32, (8, HD), 1)
    pick = jnp.where((pick_lane // 32 == pick_row) & (pick_lane % 32 < 3), 1.0, 0.0).astype(BF16)
    rd_buf[x] = dot_nt(pick, r_own[...])

    def rd_copy(d):
        return remote(rd_buf.at[x], rd_buf.at[x], rd_send.at[d], rd_recv.at[d], at_x(d))

    for d in range(1, NX):
        rd_copy(d).start()

    def pair_offsets(p):
        return [(2 * p + e - y + 2 * NY) % NY for e in (0, 1)]

    def near_pair(i):
        rel = i + i // 2 - 2 * (i // 3) if NP == 4 else i
        return (yh + rel) % NP

    def own_blocks(kind, chunk, i):
        p = near_pair(i)
        for d in pair_offsets(p):
            y_arrived(kind, d)
        chunk(core * NP + p)

    def other_blocks(kind, chunk, i):
        if NC == 2:
            p = near_pair(i)
            for d in pair_offsets(p):
                core_arrived(kind, d)
            chunk((NC - 1 - core) * NP + p)

    def skewed(kind, chunk):
        def body(i, carry):
            own_blocks(kind, chunk, i)
            other_blocks(kind, chunk, i - 1)
            return carry

        return body

    if NP > 1:
        own_blocks(0, score_chunk, 1)
        lax.fori_loop(2, NP, skewed(0, score_chunk), 0)
        other_blocks(0, score_chunk, NP - 1)
    for xs in range(NX):
        top = m_buf[0, xs]
        for j in range(1, NJ):
            top = jnp.maximum(top, m_buf[j, xs])
        total = l_buf[0, xs] * jnp.exp2(m_buf[0, xs] - top)
        for j in range(1, NJ):
            total = total + l_buf[j, xs] * jnp.exp2(m_buf[j, xs] - top)
        st[x, xs, 0:1, :] = top
        st[x, xs, 1:2, :] = total

    def st_copy(d):
        return remote(st.at[x], st.at[x], st_send.at[d], st_recv.at[d], at_x(d))

    for d in range(1, NX):
        st_copy(d).start()

    for dx in range(1, NX):
        x_whole(1, dx).wait_recv()
    for xs in range(NX):
        gt_buf[xs] = side_by_side(1, xs)
    for d in range(1, NX):
        ref = rd_buf.at[(x + NX - d) % NX]
        remote(ref, ref, rd_send.at[d], rd_recv.at[d], at_x(d)).wait_recv()
    for b in range(NC * NY):
        kt_buf[:, b * T:(b + 1) * T] = kv[0, b].T

    def dprobs_chunk(j):
        for xs in range(NX):
            rowdot = jnp.concatenate([rd_buf[xs, h:h + 1, :] for h in range(GROUP)], axis=1)
            dp_buf[j, xs] = dot_nn(key_rows(1, j), gt_buf[xs]) - rowdot

    y_arrived(1, mate)
    dprobs_chunk(core * NP + yh)
    lax.fori_loop(1, NP, skewed(1, dprobs_chunk), 0)
    other_blocks(1, dprobs_chunk, NP - 1)
    for d in range(1, NX):
        ref = st.at[(x + NX - d) % NX]
        remote(ref, ref, st_send.at[d], st_recv.at[d], at_x(d)).wait_recv()
    for xs in range(NX):
        top = st[0, xs, 0:1, :]
        for other in range(1, NX):
            top = jnp.maximum(top, st[other, xs, 0:1, :])
        total = jnp.zeros((1, GROUP * T), F32)
        for other in range(NX):
            total = total + st[other, xs, 1:2, :] * jnp.exp2(st[other, xs, 0:1, :] - top)
        lse[xs] = top + jnp.log2(total)

    for j in range(NJ):
        for xs in range(NX):
            m_buf[j, xs] = jnp.exp2(m_buf[j, xs] - lse[xs])

    def sib_copy(kind, p):
        return remote(sib_send.at[kind, p], sib_recv.at[kind, p], sb_send.at[kind, p], sb_recv.at[kind, p], sibling)

    def y_copy(kind, p, half_of):
        d = (2 * p + half_of - y + 2 * NY) % NY
        src = y_send.at[kind, p, pl.ds(pl.multiple_of(half_of * T, T), T), :]
        return remote(src, y_recv.at[kind, d], yd_send.at[kind, d], yd_recv.at[kind, d], at_y(d))

    def key_chunk(j):
        part = jnp.zeros((2 * T, HD), F32)
        for xs in range(NX):
            ds = (e_buf[j, xs] * m_buf[j, xs] * dp_buf[j, xs]).astype(BF16)
            ds_buf[xs, j] = ds
            part = part + dot_nn(ds, stacked(0, xs))
        return part

    def value_chunk(j):
        part = jnp.zeros((2 * T, HD), F32)
        for xs in range(NX):
            part = part + dot_nn((e_buf[j, xs] * m_buf[j, xs]).astype(BF16), stacked(1, xs))
        return part

    def all_pairs(kind, chunk):
        def for_sibling(i, carry):
            p = near_pair(NP - 1 - i)
            sib_send[kind, p] = chunk((NC - 1 - core) * NP + p).astype(BF16)
            sib_copy(kind, p).start()
            return carry

        def own_pair(p):
            part = chunk(core * NP + p)
            if NC == 2:
                sib_copy(kind, p).wait_recv()
                part = part + sib_recv[kind, p].astype(F32)
            y_send[kind, p] = part.astype(BF16)
            return part

        def far_pair(i, carry):
            p = near_pair(NP - 1 - i)
            own_pair(p)
            y_copy(kind, p, 0).start()
            y_copy(kind, p, 1).start()
            return carry

        if NC == 2:
            lax.fori_loop(0, NP, for_sibling, 0)
        lax.fori_loop(0, NP - 1, far_pair, 0)
        own_dkv[kind] = own_pair(yh)
        y_copy(kind, yh, 1 - yl).start()

    all_pairs(0, key_chunk)

    def dq_copy(d):
        to = (x + d) % NX
        return remote(dq_send.at[to], dq_recv.at[d], xd_send.at[d], xd_recv.at[d], at_x(d))

    def query_block(xs):
        return dot_nn(kt_buf[...], ds_buf[xs].reshape(NJ * 2 * T, GROUP * T))

    for d in (2, 1, 3):
        to = (x + d) % NX
        dq_send[to] = query_block(to).astype(BF16)
        dq_copy(d).start()
    dq_own[...] = query_block(x)

    all_pairs(1, value_chunk)

    if NZ > 1:
        for kind, ref in enumerate((
            k_in.at[:, pl.ds(0, (NZ - 1) * HD)],
            v_in.at[:, pl.ds(0, (NZ - 1) * HD)],
            q_in.at[:, pl.ds(0, (NZ - 1) * W)],
            g_in.at[:, pl.ds(0, (NZ - 1) * W)],
            r_buf.at[pl.ds(0, NZ - 1)],
        )):
            remote(ref, ref, a_send.at[kind], a_recv.at[kind, 1], at_z(1)).wait_send()
    for kind in (0, 1):
        for dx in range(1, NX):
            x_whole(kind, dx).wait_send()
        ref = kv_block(kind, 0, core)
        for d in range(1, NY):
            remote(ref, ref, kv_send.at[kind, d], kv_recv.at[kind, d], at_y(d)).wait_send()
        if NC == 2:
            for d in range(NY):
                core_copy(kind, d).wait_send()
            for p in range(NP):
                sib_copy(kind, p).wait_send()
    for d in range(1, NX):
        rd_copy(d).wait_send()
        st_copy(d).wait_send()
        dq_copy(d).wait_send()

    def out_copy(kind, d):
        to = (z + d) % NZ
        src, dst = {
            0: (dq_fin.at[zrow(to), :], q_out.at[:, zcol(z, W)]),
            1: (dkv_fin.at[0, zrow(to), :], k_out.at[:, zcol(z, HD)]),
            2: (dkv_fin.at[1, zrow(to), :], v_out.at[:, zcol(z, HD)]),
        }[kind]
        if d == 0:
            return pltpu.make_async_copy(src, dst, zl_sem.at[kind])
        return remote(src, dst, zo_send.at[kind], zo_recv.at[kind], at_z(d))

    def out_whole(kind):
        ref = (q_out.at[:, pl.ds(0, (NZ - 1) * W)], k_out.at[:, pl.ds(0, (NZ - 1) * HD)], v_out.at[:, pl.ds(0, (NZ - 1) * HD)])[kind]
        return remote(ref, ref, zo_send.at[kind], zo_recv.at[kind], at_z(1))

    own_rows = pl.ds(pl.multiple_of(yl * T, T), T)

    dq = dq_own[...]
    for d in range(1, NX):
        ref = dq_recv.at[d]
        remote(ref, ref, xd_send.at[d], xd_recv.at[d], at_x(d)).wait_recv()
        dq = dq + dq_recv[d].astype(F32)
    dq = dq * INV_ROOT
    for h in range(GROUP):
        dq_fin[:, h * HD:(h + 1) * HD] = dq[:, h * T:(h + 1) * T].T.astype(BF16)
    for d in z_order:
        out_copy(0, d).start()
    for kind, factor in ((0, INV_ROOT), (1, 1.0)):
        total = own_dkv[kind, own_rows, :]
        for d in range(1, NY):
            ref = y_recv.at[kind, d]
            remote(ref, ref, yd_send.at[kind, d], yd_recv.at[kind, d], at_y(d)).wait_recv()
            total = total + y_recv[kind, d].astype(F32)
        dkv_fin[kind] = (total * factor).astype(BF16)
        for d in z_order:
            out_copy(1 + kind, d).start()

    for d in range(1, NY):
        for kind in (0, 1):
            ref = y_recv.at[kind, d]
            remote(ref, ref, yd_send.at[kind, d], yd_recv.at[kind, d], at_y(d)).wait_send()
    for kind in range(3):
        out_copy(kind, 0).wait()
        if NZ > 1:
            out_whole(kind).wait()


def copy_kernel(q_from, k_from, v_from, q_to, k_to, v_to, sem):
    copies = [
        pltpu.make_async_copy(q_from, q_to, sem.at[0]),
        pltpu.make_async_copy(k_from, k_to, sem.at[1]),
        pltpu.make_async_copy(v_from, v_to, sem.at[2]),
    ]
    for copy in copies:
        copy.start()
    for copy in copies:
        copy.wait()


def on_device(queries, keys, values, outputs, grad_out, span_order):
    T = NZ * ROWS
    NJ = NC * NY // 2
    NP = NY // 2
    vmem = pltpu.VMEM
    dma = pltpu.SemaphoreType.DMA
    width = W * NZ
    kv_width = HD * NZ
    scratch = [
        vmem((ROWS, width), BF16),
        vmem((ROWS, width), BF16),
        vmem((NZ, ROWS, HD), BF16),
        vmem((T, HD), BF16),
        vmem((NX, 8, T), F32),
        vmem((2, NX, T, W), BF16),
        vmem((2, NC * NY, T, HD), BF16),
        vmem((NC * NY, T, HD), jnp.int32),
        vmem((8, T), jnp.int32),
        vmem((NX, HD, GROUP * T), BF16),
        vmem((NX, HD, GROUP * T), BF16),
        vmem((HD, NC * NY * T), BF16),
        vmem((NJ, NX, 2 * T, GROUP * T), F32),
        vmem((NJ, NX, 2 * T, GROUP * T), F32),
        vmem((NX, NJ, 2 * T, GROUP * T), BF16),
        vmem((NJ, NX, 1, GROUP * T), F32),
        vmem((NJ, NX, 1, GROUP * T), F32),
        vmem((NX, NX, 2, GROUP * T), F32),
        vmem((NX, 1, GROUP * T), F32),
        vmem((HD, GROUP * T), F32),
        vmem((NX, HD, GROUP * T), BF16),
        vmem((NX, HD, GROUP * T), BF16),
        vmem((2, NP, 2 * T, HD), BF16),
        vmem((2, NP, 2 * T, HD), BF16),
        vmem((2, NP, 2 * T, HD), BF16),
        vmem((2, NY, T, HD), BF16),
        vmem((2, 2 * T, HD), F32),
        vmem((T, W), BF16),
        vmem((2, T, HD), BF16),
        dma((6,)),
        dma((5,)), dma((5, NZ)),
        dma((2, NX)), dma((2, NX)),
        dma((NX,)), dma((NX,)),
        dma((2, NY)), dma((2, NY)),
        dma((2, NY)), dma((2, NY)),
        dma((NX,)), dma((NX,)),
        dma((2, NP)), dma((2, NP)),
        dma((2, NY)), dma((2, NY)),
        dma((NX,)), dma((NX,)),
        dma((3,)), dma((3,)), dma((3,)),
    ]
    anywhere = pl.BlockSpec(memory_space=pl.ANY)
    in_vmem = pl.BlockSpec(memory_space=pltpu.VMEM)
    shapes = (
        jax.ShapeDtypeStruct((ROWS, width), BF16),
        jax.ShapeDtypeStruct((ROWS, kv_width), BF16),
        jax.ShapeDtypeStruct((ROWS, kv_width), BF16),
    )
    grads = pl.pallas_call(
        kernel,
        out_shape=shapes,
        in_specs=[anywhere] * 5 + [pl.BlockSpec(memory_space=pltpu.SMEM)],
        out_specs=(in_vmem, in_vmem, in_vmem),
        scratch_shapes=scratch,
        compiler_params=pltpu.CompilerParams(
            collective_id=0, has_side_effects=True, vmem_limit_bytes=56 * 1024 * 1024
        ),
    )(queries, keys, values, outputs, grad_out, span_order)
    return pl.pallas_call(
        copy_kernel,
        out_shape=shapes,
        in_specs=[in_vmem, in_vmem, in_vmem],
        out_specs=(anywhere, anywhere, anywhere),
        scratch_shapes=[dma((3,))],
    )(*grads)


def solution(mesh):
    rows = P(("blk", "head"), None)
    return jax.shard_map(
        on_device,
        mesh=mesh,
        in_specs=(rows, rows, rows, rows, rows, P()),
        out_specs=(rows, rows, rows),
        check_vma=False,
    )
```
